32 devices in a mesh: lat: 8 (over z, x), lon: 4 (over y, core).
Axes of the slice: x: 2, y: 2, z: 4, core: 2. Of those that a mesh axis runs over, the one named last changes fastest.
Arguments:
- fields: bfloat16 [4, 48, 48, 384], P(None, 'lat', 'lon'), may hold values from -6 to 6
- cotangent: bfloat16 [4, 48, 48, 384], P(None, 'lat', 'lon'), may hold values from -6 to 6
- window_mask: int32 [2, 8, 4], P(None, 'lat', 'lon'), may hold values 0 or 1
- mask_token: bfloat16 [384], replicated, may hold values from -4 to 4
- norm_gain: bfloat16 [384], replicated, may hold values from 0.5 to 1.5
- qkv_weight: bfloat16 [1152, 384], replicated, may hold values from -0.3125 to 0.3125
- out_weight: bfloat16 [384, 384], replicated, may hold values from -0.3125 to 0.3125
- bias_table: float32 [8, 12, 759], P('lat'), may hold values from -300 to 300
- bias_index: int32 [144, 144], replicated, may hold values from 0 to 758
Outputs:
- output: bfloat16 [4, 48, 48, 384], P(None, 'lat', 'lon')
- input_grad: bfloat16 [4, 48, 48, 384], P(None, 'lat', 'lon')
- weight_grads: float32 [1536, 384], P(('lat', 'lon'))
- table_grad: float32 [8, 12, 759], P('lat')
- vector_grads: float32 [2, 384], replicated
The draws below stay inside these ranges and needn't reach their ends.
All inputs are finite; a program needn't handle non-finite values. No bound on the sum of `window_mask` on one device may be relied on, other than what follows from the above.
Results may differ from the reference program's by a relative error of at most 0.02.
Values may be sent and summed in bfloat16 or wider, within the bound.
A program may use at most 64 MiB of HBM per device.

```python
import jax
import jax.numpy as jnp
from jax import lax

D = 384
HEADS = 12
HEAD_DIM = 32
WIN_Z = 2
WIN_LAT = 6
WIN_LON = 12
WIN_TOK = 144
NBIAS = 759
LEVELS = 4
NLAT = 48
NLON = 48
LAT_WIN = 8


def draw_bias_table(key, part):
    key = jax.random.fold_in(key, 7)
    shape = (LAT_WIN, HEADS, NBIAS)
    return jax.random.normal(key, shape, jnp.float32)


def touch_ends(result, key, low, largest):
    longest = result.shape.index(max(result.shape))
    spots = []
    for shift in (0, 1):
        where = [jax.random.randint(jax.random.fold_in(key, axis), (), 0, length) for axis, length in enumerate(result.shape)]
        where[longest] = (where[longest] + shift) % result.shape[longest]
        spots.append(tuple(where))
    return result.at[spots[0]].set(low).at[spots[1]].set(largest)


def level_of(rng, shape, cuts, low, largest):
    loudness = 1.0
    for dim, shards_of in cuts:
        heights = jax.random.uniform(jax.random.fold_in(jax.random.fold_in(rng, 6), dim), (shards_of,), jnp.float32, low / len(cuts), largest / len(cuts))
        loudness = loudness * jnp.repeat(jnp.exp(heights), shape[dim] // shards_of).reshape((-1,) + (1,) * (len(shape) - 1 - dim))
    return loudness


def normal_values(rng, shape, width, limit, cuts=(), held_as=jnp.bfloat16):
    values = jax.random.normal(rng, shape, jnp.float32) * width
    if len(cuts) > 0:
        values = level_of(rng, shape, cuts, -0.22, 0.18) * values
    return jnp.clip(values, min=-limit, max=limit).astype(held_as)


def setup_inputs(seed: int = 0) -> dict:
    seeds = jax.random.split(jax.random.key(seed), 10)
    fields = normal_values(seeds[0], (LEVELS, NLAT, NLON, D), 1.0, 6.0, ((1, 8), (2, 4)))
    cotangent = normal_values(seeds[1], (LEVELS, NLAT, NLON, D), 1.0, 6.0, ((1, 8), (2, 4)))
    window_mask = touch_ends((jax.random.randint(seeds[2], (LEVELS // WIN_Z, NLAT // WIN_LAT, NLON // WIN_LON), 0, 2) < 1).astype(jnp.int32), jax.random.fold_in(seeds[2], 1), 0, 1)
    mask_token = normal_values(seeds[3], (D,), 1.0, 4.0)
    norm_gain = jnp.clip(1.0 + 0.1 * jax.random.normal(seeds[4], (D,), jnp.float32), 0.5, 1.5).astype(jnp.bfloat16)
    qkv_weight = normal_values(seeds[5], (3 * D, D), D ** -0.5, 0.3125)
    out_weight = normal_values(seeds[6], (D, D), D ** -0.5, 0.3125)
    bias_table = draw_bias_table(jax.random.fold_in(seeds[9], 71), 0)
    bias_index = touch_ends(jax.random.randint(seeds[8], (WIN_TOK, WIN_TOK), 0, NBIAS), jax.random.fold_in(seeds[8], 1), 0, NBIAS - 1).astype(jnp.int32)
    return dict(fields=fields, cotangent=cotangent, window_mask=window_mask, mask_token=mask_token, norm_gain=norm_gain, qkv_weight=qkv_weight, out_weight=out_weight, bias_table=bias_table, bias_index=bias_index)


EPS = 1e-05
BLOCKED = -10000.0

def expand_mask(window_mask):
    spread = jnp.repeat(window_mask, WIN_Z, axis=0)
    spread = jnp.repeat(spread, WIN_LAT, axis=1)
    return jnp.repeat(spread, WIN_LON, axis=2)

def region_of(coords, extent, window):
    return (coords >= extent - window).astype(jnp.int32) + (coords >= extent - window // 2).astype(jnp.int32)

def to_windows(value):
    level_count, row_count, col_count, chan_count = value.shape
    value = value.reshape(level_count // WIN_Z, WIN_Z, row_count // WIN_LAT, WIN_LAT, col_count // WIN_LON, WIN_LON, chan_count)
    value = value.transpose(2, 0, 4, 1, 3, 5, 6)
    return value.reshape(row_count // WIN_LAT, level_count // WIN_Z * (col_count // WIN_LON), WIN_TOK, chan_count)

def from_windows(value, level_count, col_count):
    row_groups = value.shape[0]
    chan_count = value.shape[3]
    value = value.reshape(row_groups, level_count // WIN_Z, col_count // WIN_LON, WIN_Z, WIN_LAT, WIN_LON, chan_count)
    value = value.transpose(1, 3, 0, 4, 2, 5, 6)
    return value.reshape(level_count, row_groups * WIN_LAT, col_count, chan_count)

def window_block(tokens_win, cot_win, bias, regions, qkv_weight, out_weight):
    wide = jnp.float32
    low = jnp.bfloat16
    groups = tokens_win.shape[0]
    members = tokens_win.shape[1]
    scale = HEAD_DIM ** (-0.5)
    projected = jnp.einsum('rmtd,fd->rmtf', tokens_win.astype(wide), qkv_weight.astype(wide)).astype(low)
    projected = projected.reshape(groups, members, WIN_TOK, 3, HEADS, HEAD_DIM)
    queries = projected[:, :, :, 0]
    key_rows = projected[:, :, :, 1]
    values = projected[:, :, :, 2]
    scores = jnp.einsum('rmthe,rmshe->rmhts', queries.astype(wide), key_rows.astype(wide)) * scale + bias[:, None]
    apart = regions[:, :, :, None] != regions[:, :, None, :]
    scores = jnp.where(apart[:, :, None], BLOCKED, scores)
    row_max = lax.optimization_barrier(jnp.max(scores, axis=-1, keepdims=True))
    exponent = jnp.exp(scores - row_max)
    attn_prob = (exponent / lax.optimization_barrier(jnp.sum(exponent, axis=-1, keepdims=True))).astype(low)
    mixed_heads = jnp.einsum('rmhts,rmshe->rmthe', attn_prob.astype(wide), values.astype(wide)).astype(low)
    mixed_heads = mixed_heads.reshape(groups, members, WIN_TOK, HEADS * HEAD_DIM)
    branch = jnp.einsum('rmtd,fd->rmtf', mixed_heads.astype(wide), out_weight.astype(wide)).astype(low)
    out_grad = jnp.einsum('rmtf,rmtd->fd', cot_win.astype(wide), mixed_heads.astype(wide))
    grad_mixed = jnp.einsum('rmtf,fd->rmtd', cot_win.astype(wide), out_weight.astype(wide)).astype(low)
    grad_mixed = grad_mixed.reshape(groups, members, WIN_TOK, HEADS, HEAD_DIM)
    grad_attn = jnp.einsum('rmthe,rmshe->rmhts', grad_mixed.astype(wide), values.astype(wide))
    grad_values = jnp.einsum('rmhts,rmthe->rmshe', attn_prob.astype(wide), grad_mixed.astype(wide)).astype(low)
    prob_float = attn_prob.astype(wide)
    grad_scores = prob_float * (grad_attn - lax.optimization_barrier(jnp.sum(prob_float * grad_attn, axis=-1, keepdims=True)))
    bias_grad = lax.optimization_barrier(jnp.sum(grad_scores, axis=1))
    scores_low = grad_scores.astype(low)
    grad_queries = (jnp.einsum('rmhts,rmshe->rmthe', scores_low.astype(wide), key_rows.astype(wide)) * scale).astype(low)
    grad_keys = (jnp.einsum('rmhts,rmthe->rmshe', scores_low.astype(wide), queries.astype(wide)) * scale).astype(low)
    grad_qkv = jnp.stack((grad_queries, grad_keys, grad_values), axis=3).reshape(groups, members, WIN_TOK, 3 * HEADS * HEAD_DIM)
    qkv_grad = jnp.einsum('rmtf,rmtd->fd', grad_qkv.astype(wide), tokens_win.astype(wide))
    grad_tokens = jnp.einsum('rmtf,fd->rmtd', grad_qkv.astype(wide), qkv_weight.astype(wide)).astype(low)
    return (branch, grad_tokens, qkv_grad, out_grad, bias_grad)

def reference(fields, cotangent, window_mask, mask_token, norm_gain, qkv_weight, out_weight, bias_table, bias_index):
    wide = jnp.float32
    masked = expand_mask(window_mask) == 1
    filled = jnp.where(masked[..., None], mask_token, fields)
    filled_wide = filled.astype(wide)
    center = filled_wide - lax.optimization_barrier(jnp.mean(filled_wide, axis=-1, keepdims=True))
    inv_std = lax.rsqrt(lax.optimization_barrier(jnp.mean(center * center, axis=-1, keepdims=True)) + EPS)
    standard = center * inv_std
    normed = (standard * norm_gain.astype(wide)).astype(jnp.bfloat16)
    offsets = (-(WIN_Z // 2), -(WIN_LAT // 2), -(WIN_LON // 2))
    backs = (WIN_Z // 2, WIN_LAT // 2, WIN_LON // 2)
    shifted = jnp.roll(normed, offsets, axis=(0, 1, 2))
    shifted_cot = jnp.roll(cotangent, offsets, axis=(0, 1, 2))
    level_ids = region_of(jnp.arange(LEVELS, dtype=jnp.int32), LEVELS, WIN_Z)
    lat_ids = region_of(jnp.arange(NLAT, dtype=jnp.int32), NLAT, WIN_LAT)
    regions = level_ids[:, None] * 3 + lat_ids[None, :]
    region_field = jnp.broadcast_to(regions[:, :, None, None], (LEVELS, NLAT, NLON, 1))
    region_win = to_windows(region_field)[..., 0]
    bias = jnp.take(bias_table, bias_index.reshape(-1), axis=2).reshape(LAT_WIN, HEADS, WIN_TOK, WIN_TOK)

    def one_row(items):
        tokens_row, cot_row, bias_row, region_row = items
        outs = window_block(tokens_row[None], cot_row[None], bias_row[None], region_row[None], qkv_weight, out_weight)
        return (outs[0][0], outs[1][0], outs[2], outs[3], outs[4][0])
    branch_win, grad_win, qkv_parts, out_parts, bias_grad = lax.map(one_row, (to_windows(shifted), to_windows(shifted_cot), bias, region_win))
    qkv_grad = lax.optimization_barrier(jnp.sum(qkv_parts, axis=0))
    out_grad = lax.optimization_barrier(jnp.sum(out_parts, axis=0))
    branch = jnp.roll(from_windows(branch_win, LEVELS, NLON), backs, axis=(0, 1, 2))
    grad_normed = jnp.roll(from_windows(grad_win, LEVELS, NLON), backs, axis=(0, 1, 2))
    output = (filled_wide + branch.astype(wide)).astype(jnp.bfloat16)
    scaled = grad_normed.astype(wide) * norm_gain.astype(wide)
    grad_filled = cotangent.astype(wide) + inv_std * (scaled - lax.optimization_barrier(jnp.mean(scaled, axis=-1, keepdims=True)) - standard * lax.optimization_barrier(jnp.mean(scaled * standard, axis=-1, keepdims=True)))
    input_grad = jnp.where(masked[..., None], 0.0, grad_filled).astype(jnp.bfloat16)
    gain_grad = lax.optimization_barrier(jnp.sum(grad_normed.astype(wide) * standard, axis=(0, 1, 2)))
    token_grad = lax.optimization_barrier(jnp.sum(jnp.where(masked[..., None], grad_filled, 0.0), axis=(0, 1, 2)))
    vector_grads = jnp.stack((gain_grad, token_grad))
    flat_grad = bias_grad.reshape(LAT_WIN * HEADS, WIN_TOK * WIN_TOK).T
    table_grad = jax.ops.segment_sum(flat_grad, bias_index.reshape(-1), num_segments=NBIAS).T.reshape(LAT_WIN, HEADS, NBIAS)
    weight_grads = jnp.concatenate((qkv_grad, out_grad), axis=0)
    return (output, input_grad, weight_grads, table_grad, vector_grads)
```

```python
import functools

import jax
import jax.numpy as jnp
from jax import lax
from jax.experimental import pallas as pl
from jax.experimental.pallas import tpu as pltpu
from jax.sharding import PartitionSpec as P

D = 384
HEADS = 12
HEAD_DIM = 32
NBIAS = 759
EPS = 1e-05
BLOCKED = -10000.0
NEVER = -1e30

PIECE = 36
PADDED = 40
TOK = 4 * PADDED
QUAD = 2 * PADDED
CHUNKS = 6
LANES = 128
ROWS = 16

WIDE = jnp.float32
LOW = jnp.bfloat16
VMEM = pl.BlockSpec(memory_space=pltpu.VMEM)
SMEM = pl.BlockSpec(memory_space=pltpu.SMEM)
PARAMS = pltpu.CompilerParams(vmem_limit_bytes=48 * 1024 * 1024)


def nn(a, b):
    return lax.dot_general(a, b, (((1,), (0,)), ((), ())), preferred_element_type=WIDE)


def nt(a, b):
    return lax.dot_general(a, b, (((1,), (1,)), ((), ())), preferred_element_type=WIDE)


def tn(a, b):
    return lax.dot_general(a, b, (((0,), (0,)), ((), ())), preferred_element_type=WIDE)


def places():
    for level in range(4):
        shifted = (level - 1) % 4
        for row in range(6):
            yield level, row, row // 3, (shifted // 2) * PADDED + (shifted % 2) * 18 + (row % 3) * 6


def pack_kernel(mask_ref, fields_ref, cot_ref, q0, q1, q2, q3, held):
    for quad in range(4):
        for win in range(2):
            start = win * PADDED + PIECE - 4
            held[quad, start : start + 8, :] = jnp.zeros((8, 2 * D), WIDE)
    for level, row, half, start in places():
        for part, ref in enumerate((fields_ref, cot_ref)):
            value = ref[level, row].astype(WIDE)
            lanes = slice(part * D, part * D + D)
            held[2 * half, start : start + 6, lanes] = value[0:6]
            held[2 * half + 1, start : start + 6, lanes] = value[6:12]
    low = mask_ref[0, 0, 0].astype(WIDE)
    high = mask_ref[1, 0, 0].astype(WIDE)
    for quad in range(4):
        for win, (first, second) in enumerate(((low, high), (high, low))):
            start = win * PADDED + PIECE
            held[quad, start : start + 1, :] = jnp.full((1, 2 * D), first)
            held[quad, start + 1 : start + 2, :] = jnp.full((1, 2 * D), second)
    for quad, ref in enumerate((q0, q1, q2, q3)):
        ref[...] = held[quad].astype(LOW)


def unpack_kernel(q0, q1, q2, q3, output_ref, grad_ref, held):
    for quad, ref in enumerate((q0, q1, q2, q3)):
        held[quad] = ref[...].astype(WIDE)
    for level, row, half, start in places():
        for part, ref in enumerate((output_ref, grad_ref)):
            lanes = slice(part * D, part * D + D)
            left = held[2 * half, start : start + 6, lanes]
            right = held[2 * half + 1, start : start + 6, lanes]
            ref[level, row] = jnp.concatenate((left, right), axis=0).astype(LOW)


def token_of(place):
    quad = place // PADDED
    within = place % PADDED
    level = within // 18
    row = (within % 18) // 6 + (quad // 2) * 3
    col = within % 6 + (quad % 2) * 6
    return jnp.where(within < PIECE, level * 72 + row * 12 + col, -1)


def lookup_kernel(table_ref, index_ref, bias_ref, place_ref):
    rows = lax.broadcasted_iota(jnp.int32, (TOK, 144), 0)
    pick_rows = (token_of(rows) == lax.broadcasted_iota(jnp.int32, (TOK, 144), 1)).astype(WIDE).astype(LOW)
    cols = lax.broadcasted_iota(jnp.int32, (2 * LANES, 144), 0)
    cols = jnp.where(cols < TOK, token_of(cols), -1)
    pick_cols = (cols == lax.broadcasted_iota(jnp.int32, (2 * LANES, 144), 1)).astype(WIDE).astype(LOW)
    index = index_ref[...]
    high = (index >> 7).astype(WIDE).astype(LOW)
    low = (index & 127).astype(WIDE).astype(LOW)
    high = nt(nn(pick_rows, high).astype(LOW), pick_cols).astype(jnp.int32)
    low = nt(nn(pick_rows, low).astype(LOW), pick_cols).astype(jnp.int32)
    place_ref[...] = high * LANES + low
    for half in range(2):
        lanes = slice(half * LANES, half * LANES + LANES)

        def block(step, carry, lanes=lanes):
            span = pl.ds(pl.multiple_of(step * 8, 8), 8)
            place = place_ref[span, lanes]
            chunk = place >> 7
            lane = place & 127
            for head in range(HEADS):
                total = jnp.zeros((8, LANES), WIDE)
                for c in range(CHUNKS):
                    row = table_ref[head : head + 1, c * LANES : c * LANES + LANES]
                    got = jnp.take_along_axis(jnp.broadcast_to(row, (8, LANES)), lane, axis=1)
                    total = jnp.where(chunk == c, got, total)
                bias_ref[head, span, lanes] = total
            return carry

        lax.fori_loop(0, TOK // 8, block, 0)


def window_kernel(
    place_ref,
    q0,
    q1,
    q2,
    q3,
    token_ref,
    gain_ref,
    qkv_w_ref,
    out_w_ref,
    bias_ref,
    y0,
    y1,
    y2,
    y3,
    wgrad_ref,
    vgrad_ref,
    pair_ref,
    qkv_s,
    gm_s,
    mixed_s,
    gqkv_s,
):
    scale = HEAD_DIM ** (-0.5)
    pieces = [ref[...].astype(WIDE) for ref in (q0, q1, q2, q3)]

    def gathered(lanes):
        return jnp.concatenate(
            [pieces[q][w * PADDED : w * PADDED + PADDED, lanes] for w in range(2) for q in range(4)], axis=0
        )

    spot = lax.broadcasted_iota(jnp.int32, (PADDED, 1), 0)
    marks = []
    for win in range(2):
        for quad in range(4):
            start = win * PADDED + PIECE
            first = pieces[quad][start : start + 1, 0:1]
            second = pieces[quad][start + 1 : start + 2, 0:1]
            marks.append(
                jnp.where(spot < 18, first, 0.0) + jnp.where((spot >= 18) & (spot < PIECE), second, 0.0)
            )
    masked = jnp.concatenate(marks, axis=0) > 0.5
    real = (lax.broadcasted_iota(jnp.int32, (2 * TOK, 1), 0) % PADDED) < PIECE
    gain = gain_ref[...].astype(WIDE)
    filled = jnp.where(masked, token_ref[...].astype(WIDE), gathered(slice(0, D)))
    filled = jnp.where(real, filled, 0.0)
    cot_wide = jnp.where(real, gathered(slice(D, 2 * D)), 0.0)
    cot = cot_wide.astype(LOW)
    center = filled - jnp.mean(filled, axis=-1, keepdims=True)
    inv_std = lax.rsqrt(jnp.mean(center * center, axis=-1, keepdims=True) + EPS)
    standard = center * inv_std
    normed = (standard * gain).astype(LOW)
    qkv_s[...] = nt(normed, qkv_w_ref[...]).astype(LOW)
    gm_s[...] = nn(cot, out_w_ref[...]).astype(LOW)

    edge = place_ref[0] == 1
    row_at = lax.broadcasted_iota(jnp.int32, (TOK, TOK), 0)
    col_at = lax.broadcasted_iota(jnp.int32, (TOK, TOK), 1)
    pad_col = (col_at % PADDED) >= PIECE
    lat_apart = ((row_at >= TOK // 2) != (col_at >= TOK // 2)) & edge
    level_apart = ((row_at % PADDED) >= 18) != ((col_at % PADDED) >= 18)
    fills = []
    for apart in (lat_apart, lat_apart | level_apart):
        fills.append(jnp.where(pad_col, NEVER, jnp.where(apart, BLOCKED, 0.0)))
    lane_head = lax.broadcasted_iota(jnp.int32, (TOK, LANES), 1) // HEAD_DIM

    for group in range(3):
        at = group * LANES
        parts = []
        for win in range(2):
            rows = slice(win * TOK, win * TOK + TOK)
            parts.append(
                (
                    qkv_s[rows, at : at + LANES],
                    qkv_s[rows, D + at : D + at + LANES],
                    qkv_s[rows, 2 * D + at : 2 * D + at + LANES],
                    gm_s[rows, at : at + LANES],
                )
            )
        sums = [[jnp.zeros((TOK, LANES), WIDE) for _ in range(4)] for _ in range(2)]
        for member in range(4):
            head = group * 4 + member
            mine = lane_head == member
            bias = bias_ref[head, :, 0:TOK]
            pair = jnp.zeros((TOK, TOK), WIDE)
            for win in range(2):
                query, key, value, gm = parts[win]
                none = jnp.zeros_like(query)
                query = jnp.where(mine, query, none)
                value_h = jnp.where(mine, value, none)
                gm_h = jnp.where(mine, gm, none)
                key_h = jnp.where(mine, key, none)
                scores = nt(query, key) * scale + bias
                scores = jnp.where(fills[win] == 0.0, scores, fills[win])
                exponent = jnp.exp(scores - jnp.max(scores, axis=-1, keepdims=True))
                prob = (exponent / jnp.sum(exponent, axis=-1, keepdims=True)).astype(LOW)
                grad_attn = nt(gm_h, value)
                prob_wide = prob.astype(WIDE)
                weighted = prob_wide * grad_attn
                grad_scores = weighted - prob_wide * jnp.sum(weighted, axis=-1, keepdims=True)
                pair = pair + grad_scores
                low = grad_scores.astype(LOW)
                sums[win][0] += nn(prob, value_h)
                sums[win][1] += nn(low, key_h)
                sums[win][2] += tn(low, query)
                sums[win][3] += tn(prob, gm_h)
            pair_ref[head] = pair
        for win in range(2):
            rows = slice(win * TOK, win * TOK + TOK)
            mixed, gq, gk, gv = sums[win]
            mixed_s[rows, at : at + LANES] = mixed.astype(LOW)
            gqkv_s[rows, at : at + LANES] = (gq * scale).astype(LOW)
            gqkv_s[rows, D + at : D + at + LANES] = (gk * scale).astype(LOW)
            gqkv_s[rows, 2 * D + at : 2 * D + at + LANES] = gv.astype(LOW)

    mixed = mixed_s[...]
    wgrad_ref[3 * D : 4 * D, :] = tn(cot, mixed).astype(wgrad_ref.dtype)
    for part in range(3):
        wgrad_ref[part * D : part * D + D, :] = tn(gqkv_s[:, part * D : part * D + D], normed).astype(
            wgrad_ref.dtype
        )
    branch = nt(mixed, out_w_ref[...]).astype(LOW).astype(WIDE)
    output = filled + branch
    grad_normed = nn(gqkv_s[...], qkv_w_ref[...]).astype(LOW).astype(WIDE)
    scaled = grad_normed * gain
    grad_filled = cot_wide + inv_std * (
        scaled
        - jnp.mean(scaled, axis=-1, keepdims=True)
        - standard * jnp.mean(scaled * standard, axis=-1, keepdims=True)
    )
    input_grad = jnp.where(masked, 0.0, grad_filled)
    vgrad_ref[0:1, :] = jnp.sum(grad_normed * standard, axis=0, keepdims=True)
    vgrad_ref[1:2, :] = jnp.sum(jnp.where(masked, grad_filled, 0.0), axis=0, keepdims=True)
    for quad, ref in enumerate((y0, y1, y2, y3)):
        for part, value in enumerate((output, input_grad)):
            both = [value[w * TOK + quad * PADDED : w * TOK + quad * PADDED + PADDED] for w in range(2)]
            ref[:, part * D : part * D + D] = jnp.concatenate(both, axis=0).astype(LOW)


def table_kernel(pair_ref, place_ref, table_ref, turned):
    for head in range(HEADS):
        turned[:, head, :] = pair_ref[head]
    turned[:, HEADS:ROWS, :] = jnp.zeros((TOK, ROWS - HEADS, TOK), WIDE)
    lane_at = lax.broadcasted_iota(jnp.int32, (LANES, TOK), 0)

    def step(block, total):
        for inner in range(8):
            row = block * 8 + inner
            place = place_ref[pl.ds(row, 1), 0:TOK]
            chunk = place >> 7
            hot = ((place & 127) == lane_at).astype(WIDE).astype(LOW)
            grad = turned[row]
            spread = jnp.concatenate([jnp.where(chunk == c, grad, 0.0) for c in range(CHUNKS)], axis=0)
            total = total + nt(spread.astype(LOW), hot)
        return total

    total = lax.fori_loop(0, TOK // 8, step, jnp.zeros((CHUNKS * ROWS, LANES), WIDE))
    for c in range(CHUNKS):
        table_ref[:, c * LANES : c * LANES + LANES] = total[c * ROWS : c * ROWS + ROWS]


def struct(shape, dtype):
    return jax.ShapeDtypeStruct(shape, dtype)


def sent(value, lat_steps, lon_steps):
    lat_count, lon_count = lax.axis_size("lat"), lax.axis_size("lon")
    pairs = []
    for a in range(lat_count):
        for o in range(lon_count):
            to = ((a + lat_steps) % lat_count) * lon_count + (o + lon_steps) % lon_count
            pairs.append((a * lon_count + o, to))
    return lax.ppermute(value, ("lat", "lon"), pairs)


def local(
    fields,
    cotangent,
    window_mask,
    mask_token,
    norm_gain,
    qkv_weight,
    out_weight,
    bias_table,
    bias_index,
):
    quad = struct((QUAD, 2 * D), LOW)
    packed = pl.pallas_call(
        pack_kernel,
        out_shape=(quad,) * 4,
        in_specs=[SMEM, VMEM, VMEM],
        out_specs=(VMEM,) * 4,
        scratch_shapes=[pltpu.VMEM((4, QUAD, 2 * D), WIDE)],
        compiler_params=PARAMS,
        name="pack",
    )(window_mask, fields, cotangent)
    from_lon = sent(packed[2], 0, -1)
    from_lat = sent(packed[1], -1, 0)
    from_both = sent(packed[0], -1, -1)
    table = jnp.pad(bias_table[0], ((0, ROWS - HEADS), (0, CHUNKS * LANES - NBIAS)))
    bias, place = pl.pallas_call(
        lookup_kernel,
        out_shape=(struct((HEADS, TOK, 2 * LANES), WIDE), struct((TOK, 2 * LANES), jnp.int32)),
        in_specs=[VMEM, VMEM],
        out_specs=(VMEM, VMEM),
        compiler_params=PARAMS,
        cost_estimate=pl.CostEstimate(flops=4_000_000_000, bytes_accessed=8_000_000, transcendentals=0),
        name="lookup",
    )(table, bias_index)
    edge = (lax.axis_index("lat") == lax.axis_size("lat") - 1).astype(jnp.int32).reshape(1)
    y0, y1, y2, y3, wgrad, vgrad, pair = pl.pallas_call(
        window_kernel,
        out_shape=(quad,) * 4
        + (struct((4 * D, D), WIDE), struct((2, D), WIDE), struct((HEADS, TOK, TOK), WIDE)),
        in_specs=[SMEM] + [VMEM] * 9,
        out_specs=(VMEM,) * 7,
        scratch_shapes=[
            pltpu.VMEM((2 * TOK, 3 * D), LOW),
            pltpu.VMEM((2 * TOK, D), LOW),
            pltpu.VMEM((2 * TOK, D), LOW),
            pltpu.VMEM((2 * TOK, 3 * D), LOW),
        ],
        compiler_params=PARAMS,
        name="windows",
    )(
        edge,
        packed[3],
        from_lon,
        from_lat,
        from_both,
        mask_token.reshape(1, D),
        norm_gain.reshape(1, D),
        qkv_weight,
        out_weight,
        bias,
    )
    back_lon = sent(y1, 0, 1)
    back_lat = sent(y2, 1, 0)
    back_both = sent(y3, 1, 1)
    table_local = pl.pallas_call(
        table_kernel,
        out_shape=struct((ROWS, CHUNKS * LANES), WIDE),
        in_specs=[VMEM, VMEM],
        out_specs=VMEM,
        scratch_shapes=[pltpu.VMEM((TOK, ROWS, TOK), WIDE)],
        compiler_params=PARAMS,
        cost_estimate=pl.CostEstimate(flops=4_000_000_000, bytes_accessed=8_000_000, transcendentals=0),
        name="table",
    )(pair, place)
    output, input_grad = pl.pallas_call(
        unpack_kernel,
        out_shape=(struct(fields.shape, LOW), struct(fields.shape, LOW)),
        in_specs=[VMEM] * 4,
        out_specs=(VMEM, VMEM),
        scratch_shapes=[pltpu.VMEM((4, QUAD, 2 * D), WIDE)],
        compiler_params=PARAMS,
        name="unpack",
    )(back_both, back_lat, back_lon, y0)
    vector_grads = lax.psum(vgrad, ("lat", "lon"))
    table_grad = lax.psum(table_local[None, :HEADS, :NBIAS].astype(LOW), "lon").astype(WIDE)
    weight_grads = lax.psum_scatter(wgrad, ("lat", "lon"), scatter_dimension=0, tiled=True)
    return (output, input_grad, weight_grads, table_grad, vector_grads)


def solution(mesh):
    placed = (
        P(None, "lat", "lon", None),
        P(None, "lat", "lon", None),
        P(None, "lat", "lon"),
        P(),
        P(),
        P(),
        P(),
        P("lat", None, None),
        P(),
    )
    return jax.shard_map(
        local,
        mesh=mesh,
        in_specs=placed,
        out_specs=(
            P(None, "lat", "lon", None),
            P(None, "lat", "lon", None),
            P(("lat", "lon"), None),
            P("lat", None, None),
            P(),
        ),
        check_vma=False,
    )
```

```python
import functools

import jax
import jax.numpy as jnp
from jax import lax
from jax.experimental import pallas as pl
from jax.experimental.pallas import tpu as pltpu
from jax.sharding import PartitionSpec as P

D = 384
HEADS = 12
HEAD_DIM = 32
NBIAS = 759
EPS = 1e-05
BLOCKED = -10000.0
NEVER = -1e30

PIECE = 36
PADDED = 40
TOK = 4 * PADDED
QUAD = 2 * PADDED
CHUNKS = 6
LANES = 128
ROWS = 16

WIDE = jnp.float32
LOW = jnp.bfloat16
VMEM = pl.BlockSpec(memory_space=pltpu.VMEM)
SMEM = pl.BlockSpec(memory_space=pltpu.SMEM)
PARAMS = pltpu.CompilerParams(vmem_limit_bytes=48 * 1024 * 1024)


def nn(a, b):
    return lax.dot_general(a, b, (((1,), (0,)), ((), ())), preferred_element_type=WIDE)


def nt(a, b):
    return lax.dot_general(a, b, (((1,), (1,)), ((), ())), preferred_element_type=WIDE)


def tn(a, b):
    return lax.dot_general(a, b, (((0,), (0,)), ((), ())), preferred_element_type=WIDE)


def places():
    for level in range(4):
        shifted = (level - 1) % 4
        for row in range(6):
            yield level, row, row // 3, (shifted // 2) * PADDED + (shifted % 2) * 18 + (row % 3) * 6


def pack_kernel(mask_ref, fields_ref, cot_ref, q0, q1, q2, q3, held):
    for quad in range(4):
        for win in range(2):
            start = win * PADDED + PIECE - 4
            held[quad, start : start + 8, :] = jnp.zeros((8, 2 * D), WIDE)
    for level, row, half, start in places():
        for part, ref in enumerate((fields_ref, cot_ref)):
            value = ref[level, row].astype(WIDE)
            lanes = slice(part * D, part * D + D)
            held[2 * half, start : start + 6, lanes] = value[0:6]
            held[2 * half + 1, start : start + 6, lanes] = value[6:12]
    low = mask_ref[0, 0, 0].astype(WIDE)
    high = mask_ref[1, 0, 0].astype(WIDE)
    for quad in range(4):
        for win, (first, second) in enumerate(((low, high), (high, low))):
            start = win * PADDED + PIECE
            held[quad, start : start + 1, :] = jnp.full((1, 2 * D), first)
            held[quad, start + 1 : start + 2, :] = jnp.full((1, 2 * D), second)
    for quad, ref in enumerate((q0, q1, q2, q3)):
        ref[...] = held[quad].astype(LOW)


def token_of(place):
    quad = place // PADDED
    within = place % PADDED
    level = within // 18
    row = (within % 18) // 6 + (quad // 2) * 3
    col = within % 6 + (quad % 2) * 6
    return jnp.where(within < PIECE, level * 72 + row * 12 + col, -1)


def lookup_kernel(table_ref, index_ref, bias_ref, place_ref):
    rows = lax.broadcasted_iota(jnp.int32, (TOK, 144), 0)
    pick_rows = (token_of(rows) == lax.broadcasted_iota(jnp.int32, (TOK, 144), 1)).astype(WIDE).astype(LOW)
    cols = lax.broadcasted_iota(jnp.int32, (2 * LANES, 144), 0)
    cols = jnp.where(cols < TOK, token_of(cols), -1)
    pick_cols = (cols == lax.broadcasted_iota(jnp.int32, (2 * LANES, 144), 1)).astype(WIDE).astype(LOW)
    index = index_ref[...]
    high = (index >> 7).astype(WIDE).astype(LOW)
    low = (index & 127).astype(WIDE).astype(LOW)
    high = nt(nn(pick_rows, high).astype(LOW), pick_cols).astype(jnp.int32)
    low = nt(nn(pick_rows, low).astype(LOW), pick_cols).astype(jnp.int32)
    place_ref[...] = high * LANES + low
    for half in range(2):
        lanes = slice(half * LANES, half * LANES + LANES)

        def block(step, carry, lanes=lanes):
            span = pl.ds(pl.multiple_of(step * 8, 8), 8)
            place = place_ref[span, lanes]
            chunk = place >> 7
            lane = place & 127
            for head in range(HEADS):
                total = jnp.zeros((8, LANES), WIDE)
                for c in range(CHUNKS):
                    row = table_ref[head : head + 1, c * LANES : c * LANES + LANES]
                    got = jnp.take_along_axis(jnp.broadcast_to(row, (8, LANES)), lane, axis=1)
                    total = jnp.where(chunk == c, got, total)
                bias_ref[head, span, lanes] = total
            return carry

        lax.fori_loop(0, TOK // 8, block, 0)


def window_kernel(
    place_ref,
    q0,
    q1,
    q2,
    q3,
    token_ref,
    gain_ref,
    qkv_w_ref,
    out_w_ref,
    bias_ref,
    y0,
    y1,
    y2,
    y3,
    wgrad_ref,
    vgrad_ref,
    pair_ref,
    qkv_s,
    gm_s,
    mixed_s,
    gqkv_s,
):
    scale = HEAD_DIM ** (-0.5)
    pieces = [ref[...].astype(WIDE) for ref in (q0, q1, q2, q3)]

    def gathered(lanes):
        return jnp.concatenate(
            [pieces[q][w * PADDED : w * PADDED + PADDED, lanes] for w in range(2) for q in range(4)], axis=0
        )

    spot = lax.broadcasted_iota(jnp.int32, (PADDED, 1), 0)
    marks = []
    for win in range(2):
        for quad in range(4):
            start = win * PADDED + PIECE
            first = pieces[quad][start : start + 1, 0:1]
            second = pieces[quad][start + 1 : start + 2, 0:1]
            marks.append(
                jnp.where(spot < 18, first, 0.0) + jnp.where((spot >= 18) & (spot < PIECE), second, 0.0)
            )
    masked = jnp.concatenate(marks, axis=0) > 0.5
    real = (lax.broadcasted_iota(jnp.int32, (2 * TOK, 1), 0) % PADDED) < PIECE
    gain = gain_ref[...].astype(WIDE)
    filled = jnp.where(masked, token_ref[...].astype(WIDE), gathered(slice(0, D)))
    filled = jnp.where(real, filled, 0.0)
    cot_wide = jnp.where(real, gathered(slice(D, 2 * D)), 0.0)
    cot = cot_wide.astype(LOW)
    center = filled - jnp.mean(filled, axis=-1, keepdims=True)
    inv_std = lax.rsqrt(jnp.mean(center * center, axis=-1, keepdims=True) + EPS)
    standard = center * inv_std
    normed = (standard * gain).astype(LOW)
    qkv_s[...] = nt(normed, qkv_w_ref[...]).astype(LOW)
    gm_s[...] = nn(cot, out_w_ref[...]).astype(LOW)

    edge = place_ref[0] == 1
    row_at = lax.broadcasted_iota(jnp.int32, (TOK, TOK), 0)
    col_at = lax.broadcasted_iota(jnp.int32, (TOK, TOK), 1)
    pad_col = (col_at % PADDED) >= PIECE
    lat_apart = ((row_at >= TOK // 2) != (col_at >= TOK // 2)) & edge
    level_apart = ((row_at % PADDED) >= 18) != ((col_at % PADDED) >= 18)
    fills = []
    for apart in (lat_apart, lat_apart | level_apart):
        fills.append(jnp.where(pad_col, NEVER, jnp.where(apart, BLOCKED, 0.0)))
    lane_head = lax.broadcasted_iota(jnp.int32, (TOK, LANES), 1) // HEAD_DIM

    for group in range(3):
        at = group * LANES
        parts = []
        for win in range(2):
            rows = slice(win * TOK, win * TOK + TOK)
            parts.append(
                (
                    qkv_s[rows, at : at + LANES],
                    qkv_s[rows, D + at : D + at + LANES],
                    qkv_s[rows, 2 * D + at : 2 * D + at + LANES],
                    gm_s[rows, at : at + LANES],
                )
            )
        sums = [[jnp.zeros((TOK, LANES), WIDE) for _ in range(4)] for _ in range(2)]
        for member in range(4):
            head = group * 4 + member
            mine = lane_head == member
            bias = bias_ref[head, :, 0:TOK]
            pair = jnp.zeros((TOK, TOK), WIDE)
            for win in range(2):
                query, key, value, gm = parts[win]
                none = jnp.zeros_like(query)
                query = jnp.where(mine, query, none)
                value_h = jnp.where(mine, value, none)
                gm_h = jnp.where(mine, gm, none)
                key_h = jnp.where(mine, key, none)
                scores = nt(query, key) * scale + bias
                scores = jnp.where(fills[win] == 0.0, scores, fills[win])
                exponent = jnp.exp(scores - jnp.max(scores, axis=-1, keepdims=True))
                prob = (exponent / jnp.sum(exponent, axis=-1, keepdims=True)).astype(LOW)
                grad_attn = nt(gm_h, value)
                prob_wide = prob.astype(WIDE)
                weighted = prob_wide * grad_attn
                grad_scores = weighted - prob_wide * jnp.sum(weighted, axis=-1, keepdims=True)
                pair = pair + grad_scores
                low = grad_scores.astype(LOW)
                sums[win][0] += nn(prob, value_h)
                sums[win][1] += nn(low, key_h)
                sums[win][2] += tn(low, query)
                sums[win][3] += tn(prob, gm_h)
            pair_ref[head] = pair
        for win in range(2):
            rows = slice(win * TOK, win * TOK + TOK)
            mixed, gq, gk, gv = sums[win]
            mixed_s[rows, at : at + LANES] = mixed.astype(LOW)
            gqkv_s[rows, at : at + LANES] = (gq * scale).astype(LOW)
            gqkv_s[rows, D + at : D + at + LANES] = (gk * scale).astype(LOW)
            gqkv_s[rows, 2 * D + at : 2 * D + at + LANES] = gv.astype(LOW)

    mixed = mixed_s[...]
    wgrad_ref[3 * D : 4 * D, :] = tn(cot, mixed).astype(wgrad_ref.dtype)
    for part in range(3):
        wgrad_ref[part * D : part * D + D, :] = tn(gqkv_s[:, part * D : part * D + D], normed).astype(
            wgrad_ref.dtype
        )
    branch = nt(mixed, out_w_ref[...]).astype(LOW).astype(WIDE)
    output = filled + branch
    grad_normed = nn(gqkv_s[...], qkv_w_ref[...]).astype(LOW).astype(WIDE)
    scaled = grad_normed * gain
    grad_filled = cot_wide + inv_std * (
        scaled
        - jnp.mean(scaled, axis=-1, keepdims=True)
        - standard * jnp.mean(scaled * standard, axis=-1, keepdims=True)
    )
    input_grad = jnp.where(masked, 0.0, grad_filled)
    vgrad_ref[...] = jnp.zeros((8, D), WIDE)
    vgrad_ref[0:1, :] = jnp.sum(grad_normed * standard, axis=0, keepdims=True)
    vgrad_ref[1:2, :] = jnp.sum(jnp.where(masked, grad_filled, 0.0), axis=0, keepdims=True)
    for quad, ref in enumerate((y0, y1, y2, y3)):
        for part, value in enumerate((output, input_grad)):
            both = [value[w * TOK + quad * PADDED : w * TOK + quad * PADDED + PADDED] for w in range(2)]
            ref[:, part * D : part * D + D] = jnp.concatenate(both, axis=0).astype(LOW)


def table_sums(pair_ref, place_ref, turned):
    for head in range(HEADS):
        turned[:, head, :] = pair_ref[head]
    turned[:, HEADS:ROWS, :] = jnp.zeros((TOK, ROWS - HEADS, TOK), WIDE)
    lane_at = lax.broadcasted_iota(jnp.int32, (LANES, TOK), 0)

    def step(block, total):
        for inner in range(8):
            row = block * 8 + inner
            place = place_ref[pl.ds(row, 1), 0:TOK]
            chunk = place >> 7
            hot = ((place & 127) == lane_at).astype(WIDE).astype(LOW)
            grad = turned[row]
            spread = jnp.concatenate([jnp.where(chunk == c, grad, 0.0) for c in range(CHUNKS)], axis=0)
            total = total + nt(spread.astype(LOW), hot)
        return total

    return lax.fori_loop(0, TOK // 8, step, jnp.zeros((CHUNKS * ROWS, LANES), WIDE))


def finish_kernel(
    lat_count,
    lon_count,
    y0,
    y1,
    y2,
    y3,
    terms_ref,
    vgrad_ref,
    pair_ref,
    place_ref,
    output_ref,
    grad_ref,
    rows_ref,
    table_ref,
    vector_ref,
    landed,
    held,
    turned,
    pair_in,
    pair_sum,
    lon_in,
    lon_sum,
    lat_in,
    table_in,
    vec_in,
    vec_sum,
    vec_in_lat,
    quad_send,
    quad_recv,
    pair_send,
    pair_recv,
    lon_send,
    lon_recv,
    lat_send,
    lat_recv,
    table_send,
    table_recv,
    vec_send,
    vec_recv,
    vec_lat_send,
    vec_lat_recv,
):
    lat, lon = lax.axis_index("lat"), lax.axis_index("lon")
    half = lon_count // 2
    core, column = lon % 2, lon // 2

    def lat_at(step):
        return (lat + step + lat_count) % lat_count

    def lon_at(step):
        return (lon + step + lon_count) % lon_count

    def copy(src, dst, send_sem, recv_sem, device):
        return pltpu.make_async_remote_copy(
            src_ref=src,
            dst_ref=dst,
            send_sem=send_sem,
            recv_sem=recv_sem,
            device_id=device,
            device_id_type=pl.DeviceIdType.MESH,
        )

    barrier = pltpu.get_barrier_semaphore()
    friends = [(lat, lon_at(d)) for d in range(1, lon_count)]
    friends += [(lat_at(d), lon) for d in range(1, lat_count)]
    friends += [(lat_at(1), lon_at(1)), (lat_at(-1), lon_at(-1))]
    for friend in friends:
        pl.semaphore_signal(barrier, inc=1, device_id=friend, device_id_type=pl.DeviceIdType.MESH)
    pl.semaphore_wait(barrier, len(friends))

    pair_copy = copy(
        terms_ref.at[:, :, 1 - core], pair_in, pair_send, pair_recv, (lat, lon + 1 - 2 * core)
    )
    pair_copy.start()
    quads = [
        copy(y3, landed.at[0], quad_send.at[0], quad_recv.at[0], (lat_at(1), lon_at(1))),
        copy(y2, landed.at[1], quad_send.at[1], quad_recv.at[1], (lat_at(1), lon)),
        copy(y1, landed.at[2], quad_send.at[2], quad_recv.at[2], (lat, lon_at(1))),
    ]
    for each in quads:
        each.start()
    vec_in[lon] = vgrad_ref[...]
    vecs = []
    for d in range(1, lon_count):
        to = lon_at(d)
        vecs.append(copy(vgrad_ref, vec_in.at[lon], vec_send.at[to], vec_recv.at[lon], (lat, to)))
    for each in vecs:
        each.start()

    pair_copy.wait_recv()

    def add_pair(row, carry):
        for m in range(half):
            own = terms_ref[row, m, core].astype(WIDE)
            pair_sum[m, row] = (own + pair_in[row, m].astype(WIDE)).astype(LOW)
        return carry

    lax.fori_loop(0, lat_count, add_pair, 0)

    lon_copies = []
    for d in range(1, half):
        to = (column + d) % half
        lon_copies.append(
            copy(pair_sum.at[to], lon_in.at[column], lon_send.at[to], lon_recv.at[column], (lat, 2 * to + core))
        )
    for each in lon_copies:
        each.start()

    total = table_sums(pair_ref, place_ref, turned)
    for c in range(CHUNKS):
        table_in[lon, :, c * LANES : c * LANES + LANES] = total[c * ROWS : c * ROWS + ROWS].astype(LOW)
    tables = []
    for d in range(1, lon_count):
        to = lon_at(d)
        tables.append(copy(table_in.at[lon], table_in.at[lon], table_send.at[to], table_recv.at[lon], (lat, to)))
    for each in tables:
        each.start()

    for d in range(1, half):
        source = (column + d) % half
        copy(pair_sum.at[source], lon_in.at[source], lon_send.at[source], lon_recv.at[source], (lat, 2 * source + core)).wait_recv()

    def add_lon(row, carry):
        value = pair_sum[column, row].astype(WIDE)
        for d in range(1, half):
            value = value + lon_in[(column + d) % half, row].astype(WIDE)
        lon_sum[row] = value.astype(LOW)
        return carry

    lax.fori_loop(0, lat_count, add_lon, 0)

    lat_copies = []
    for d in range(1, lat_count):
        to = lat_at(d)
        lat_copies.append(copy(lon_sum.at[to], lat_in.at[lat], lat_send.at[to], lat_recv.at[lat], (to, lon)))
    for each in lat_copies:
        each.start()

    for d in range(1, lon_count):
        source = lon_at(d)
        copy(vgrad_ref, vec_in.at[source], vec_send.at[source], vec_recv.at[source], (lat, source)).wait_recv()
    vec = vec_in[0]
    for source in range(1, lon_count):
        vec = vec + vec_in[source]
    vec_sum[...] = vec
    vec_in_lat[lat] = vec
    vec_lats = []
    for d in range(1, lat_count):
        to = lat_at(d)
        vec_lats.append(copy(vec_sum, vec_in_lat.at[lat], vec_lat_send.at[to], vec_lat_recv.at[lat], (to, lon)))
    for each in vec_lats:
        each.start()

    for each in quads:
        each.wait_recv()
    for quad in range(3):
        held[quad] = landed[quad].astype(WIDE)
    held[3] = y0[...].astype(WIDE)
    for level, row, part_row, start in places():
        for part, ref in enumerate((output_ref, grad_ref)):
            lanes = slice(part * D, part * D + D)
            left = held[2 * part_row, start : start + 6, lanes]
            right = held[2 * part_row + 1, start : start + 6, lanes]
            ref[level, row] = jnp.concatenate((left, right), axis=0).astype(LOW)

    for d in range(1, lon_count):
        source = lon_at(d)
        copy(
            table_in.at[source], table_in.at[source], table_send.at[source], table_recv.at[source], (lat, source)
        ).wait_recv()
    table = table_in[0].astype(WIDE)
    for source in range(1, lon_count):
        table = table + table_in[source].astype(WIDE)
    table_ref[...] = table

    for d in range(1, lat_count):
        source = lat_at(d)
        copy(
            vec_sum, vec_in_lat.at[source], vec_lat_send.at[source], vec_lat_recv.at[source], (source, lon)
        ).wait_recv()
    vec = vec_in_lat[0]
    for source in range(1, lat_count):
        vec = vec + vec_in_lat[source]
    vector_ref[...] = vec

    value = lon_sum[lat].astype(WIDE)
    for d in range(1, lat_count):
        source = lat_at(d)
        copy(lon_sum.at[source], lat_in.at[source], lat_send.at[source], lat_recv.at[source], (source, lon)).wait_recv()
        value = value + lat_in[source].astype(WIDE)
    rows_ref[...] = value

    for each in [pair_copy] + quads + vecs + lon_copies + tables + lat_copies + vec_lats:
        each.wait_send()


def struct(shape, dtype):
    return jax.ShapeDtypeStruct(shape, dtype)


def sent(value, lat_steps, lon_steps):
    lat_count, lon_count = lax.axis_size("lat"), lax.axis_size("lon")
    pairs = []
    for a in range(lat_count):
        for o in range(lon_count):
            to = ((a + lat_steps) % lat_count) * lon_count + (o + lon_steps) % lon_count
            pairs.append((a * lon_count + o, to))
    return lax.ppermute(value, ("lat", "lon"), pairs)


def local(
    fields,
    cotangent,
    window_mask,
    mask_token,
    norm_gain,
    qkv_weight,
    out_weight,
    bias_table,
    bias_index,
):
    quad = struct((QUAD, 2 * D), LOW)
    packed = pl.pallas_call(
        pack_kernel,
        out_shape=(quad,) * 4,
        in_specs=[SMEM, VMEM, VMEM],
        out_specs=(VMEM,) * 4,
        scratch_shapes=[pltpu.VMEM((4, QUAD, 2 * D), WIDE)],
        compiler_params=PARAMS,
        name="pack",
    )(window_mask, fields, cotangent)
    from_lon = sent(packed[2], 0, -1)
    from_lat = sent(packed[1], -1, 0)
    from_both = sent(packed[0], -1, -1)
    table = jnp.pad(bias_table[0], ((0, ROWS - HEADS), (0, CHUNKS * LANES - NBIAS)))
    bias, place = pl.pallas_call(
        lookup_kernel,
        out_shape=(struct((HEADS, TOK, 2 * LANES), WIDE), struct((TOK, 2 * LANES), jnp.int32)),
        in_specs=[VMEM, VMEM],
        out_specs=(VMEM, VMEM),
        compiler_params=PARAMS,
        cost_estimate=pl.CostEstimate(flops=4_000_000_000, bytes_accessed=8_000_000, transcendentals=0),
        name="lookup",
    )(table, bias_index)
    edge = (lax.axis_index("lat") == lax.axis_size("lat") - 1).astype(jnp.int32).reshape(1)
    y0, y1, y2, y3, wgrad, vgrad, pair = pl.pallas_call(
        window_kernel,
        out_shape=(quad,) * 4
        + (struct((4 * D, D), LOW), struct((8, D), WIDE), struct((HEADS, TOK, TOK), WIDE)),
        in_specs=[SMEM] + [VMEM] * 9,
        out_specs=(VMEM,) * 7,
        scratch_shapes=[
            pltpu.VMEM((2 * TOK, 3 * D), LOW),
            pltpu.VMEM((2 * TOK, D), LOW),
            pltpu.VMEM((2 * TOK, D), LOW),
            pltpu.VMEM((2 * TOK, 3 * D), LOW),
        ],
        compiler_params=PARAMS,
        name="windows",
    )(
        edge,
        packed[3],
        from_lon,
        from_lat,
        from_both,
        mask_token.reshape(1, D),
        norm_gain.reshape(1, D),
        qkv_weight,
        out_weight,
        bias,
    )
    lat_count, lon_count = lax.axis_size("lat"), lax.axis_size("lon")
    half = lon_count // 2
    share = 4 * D // (lat_count * lon_count)
    output, input_grad, weight_grads, table_full, vector_full = pl.pallas_call(
        functools.partial(finish_kernel, lat_count, lon_count),
        out_shape=(
            struct(fields.shape, LOW),
            struct(fields.shape, LOW),
            struct((share, D), WIDE),
            struct((ROWS, CHUNKS * LANES), WIDE),
            struct((8, D), WIDE),
        ),
        in_specs=[VMEM] * 8,
        out_specs=(VMEM,) * 5,
        scratch_shapes=[
            pltpu.VMEM((3, QUAD, 2 * D), LOW),
            pltpu.VMEM((4, QUAD, 2 * D), WIDE),
            pltpu.VMEM((TOK, ROWS, TOK), WIDE),
            pltpu.VMEM((lat_count, half, share, D), LOW),
            pltpu.VMEM((half, lat_count, share, D), LOW),
            pltpu.VMEM((half, lat_count, share, D), LOW),
            pltpu.VMEM((lat_count, share, D), LOW),
            pltpu.VMEM((lat_count, share, D), LOW),
            pltpu.VMEM((lon_count, ROWS, CHUNKS * LANES), LOW),
            pltpu.VMEM((lon_count, 8, D), WIDE),
            pltpu.VMEM((8, D), WIDE),
            pltpu.VMEM((lat_count, 8, D), WIDE),
            pltpu.SemaphoreType.DMA((3,)),
            pltpu.SemaphoreType.DMA((3,)),
            pltpu.SemaphoreType.DMA,
            pltpu.SemaphoreType.DMA,
            pltpu.SemaphoreType.DMA((half,)),
            pltpu.SemaphoreType.DMA((half,)),
            pltpu.SemaphoreType.DMA((lat_count,)),
            pltpu.SemaphoreType.DMA((lat_count,)),
            pltpu.SemaphoreType.DMA((lon_count,)),
            pltpu.SemaphoreType.DMA((lon_count,)),
            pltpu.SemaphoreType.DMA((lon_count,)),
            pltpu.SemaphoreType.DMA((lon_count,)),
            pltpu.SemaphoreType.DMA((lat_count,)),
            pltpu.SemaphoreType.DMA((lat_count,)),
        ],
        compiler_params=pltpu.CompilerParams(
            collective_id=0, has_side_effects=True, vmem_limit_bytes=48 * 1024 * 1024
        ),
        name="finish",
    )(y0, y1, y2, y3, wgrad.reshape(lat_count, half, 2, share, D), vgrad, pair, place)
    table_grad = table_full[None, :HEADS, :NBIAS]
    vector_grads = vector_full[:2]
    return (output, input_grad, weight_grads, table_grad, vector_grads)


def solution(mesh):
    placed = (
        P(None, "lat", "lon", None),
        P(None, "lat", "lon", None),
        P(None, "lat", "lon"),
        P(),
        P(),
        P(),
        P(),
        P("lat", None, None),
        P(),
    )
    return jax.shard_map(
        local,
        mesh=mesh,
        in_specs=placed,
        out_specs=(
            P(None, "lat", "lon", None),
            P(None, "lat", "lon", None),
            P(("lat", "lon"), None),
            P("lat", None, None),
            P(),
        ),
        check_vma=False,
    )
```

```python
import functools

import jax
import jax.numpy as jnp
from jax import lax
from jax.experimental import pallas as pl
from jax.experimental.pallas import tpu as pltpu
from jax.sharding import PartitionSpec as P

D = 384
HEADS = 12
HEAD_DIM = 32
NBIAS = 759
EPS = 1e-05
BLOCKED = -10000.0
NEVER = -1e30

PIECE = 36
PADDED = 40
TOK = 4 * PADDED
QUAD = 2 * PADDED
CHUNKS = 6
LANES = 128
ROWS = 16

WIDE = jnp.float32
LOW = jnp.bfloat16
VMEM = pl.BlockSpec(memory_space=pltpu.VMEM)
SMEM = pl.BlockSpec(memory_space=pltpu.SMEM)
PARAMS = pltpu.CompilerParams(vmem_limit_bytes=32 * 1024 * 1024)


def nn(a, b):
    return lax.dot_general(a, b, (((1,), (0,)), ((), ())), preferred_element_type=WIDE)


def nt(a, b):
    return lax.dot_general(a, b, (((1,), (1,)), ((), ())), preferred_element_type=WIDE)


def tn(a, b):
    return lax.dot_general(a, b, (((0,), (0,)), ((), ())), preferred_element_type=WIDE)


def places():
    for level in range(4):
        shifted = (level - 1) % 4
        for row in range(6):
            yield level, row, row // 3, (shifted // 2) * PADDED + (shifted % 2) * 18 + (row % 3) * 6


def token_of(place):
    quad = place // PADDED
    within = place % PADDED
    level = within // 18
    row = (within % 18) // 6 + (quad // 2) * 3
    col = within % 6 + (quad % 2) * 6
    return jnp.where(within < PIECE, level * 72 + row * 12 + col, -1)


def pack(mask_ref, fields_ref, cot_ref, spread, held):
    for quad in range(4):
        for win in range(2):
            start = win * PADDED + PIECE - 4
            held[quad, start : start + 8, :] = jnp.zeros((8, 2 * D), WIDE)
    for part, ref in enumerate((fields_ref, cot_ref)):
        for row in range(6):
            for col in range(12):
                start = (row * 12 + col) * 4
                value = ref[row, col].astype(WIDE)
                for c in range(3):
                    spread[part, c, start : start + 4, :] = value[:, c * LANES : c * LANES + LANES]
        for level, row, half, start in places():
            for side in range(2):
                base = (row * 12 + side * 6) * 4 + level
                for c in range(3):
                    lanes = slice(part * D + c * LANES, part * D + c * LANES + LANES)
                    held[2 * half + side, start : start + 6, lanes] = spread[part, c, pl.ds(base, 6, stride=4), :]
    low = mask_ref[0, 0, 0].astype(WIDE)
    high = mask_ref[0, 0, 1].astype(WIDE)
    for quad in range(4):
        for win, (first, second) in enumerate(((low, high), (high, low))):
            start = win * PADDED + PIECE
            held[quad, start : start + 1, :] = jnp.full((1, 2 * D), first)
            held[quad, start + 1 : start + 2, :] = jnp.full((1, 2 * D), second)


def unpack(held, spread, output_ref, grad_ref):
    for part, ref in enumerate((output_ref, grad_ref)):
        for level, row, half, start in places():
            for side in range(2):
                base = (row * 12 + side * 6) * 4 + level
                for c in range(3):
                    lanes = slice(part * D + c * LANES, part * D + c * LANES + LANES)
                    spread[part, c, pl.ds(base, 6, stride=4), :] = held[2 * half + side, start : start + 6, lanes]
        for row in range(6):
            for col in range(12):
                start = (row * 12 + col) * 4
                value = [spread[part, c, start : start + 4, :] for c in range(3)]
                ref[row, col] = jnp.concatenate(value, axis=1).astype(LOW)


def lookup(table_ref, index_ref, bias_ref, place_ref, packed_ref):
    rows = lax.broadcasted_iota(jnp.int32, (TOK, 144), 0)
    pick_rows = (token_of(rows) == lax.broadcasted_iota(jnp.int32, (TOK, 144), 1)).astype(WIDE).astype(LOW)
    cols = lax.broadcasted_iota(jnp.int32, (2 * LANES, 144), 0)
    cols = jnp.where(cols < TOK, token_of(cols), -1)
    pick_cols = (cols == lax.broadcasted_iota(jnp.int32, (2 * LANES, 144), 1)).astype(WIDE).astype(LOW)
    index = index_ref[...]
    high = (index >> 7).astype(WIDE).astype(LOW)
    low = (index & 127).astype(WIDE).astype(LOW)
    high = nt(nn(pick_rows, high).astype(LOW), pick_cols).astype(jnp.int32)
    low = nt(nn(pick_rows, low).astype(LOW), pick_cols).astype(jnp.int32)
    place_ref[...] = high * LANES + low
    for k in range(4):
        packed_ref[:, 32 * k : 32 * k + 32] = place_ref[PADDED * k : PADDED * k + PADDED, LANES : LANES + 32]

    def found(place, head):
        chunk = place >> 7
        lane = place & 127
        total = jnp.zeros((8, LANES), WIDE)
        for c in range(CHUNKS):
            row = table_ref[head : head + 1, c * LANES : c * LANES + LANES]
            got = jnp.take_along_axis(jnp.broadcast_to(row, (8, LANES)), lane, axis=1)
            total = jnp.where(chunk == c, got, total)
        return total

    def block(step, carry):
        span = pl.ds(pl.multiple_of(step * 8, 8), 8)
        place = place_ref[span, 0:LANES]
        for head in range(HEADS):
            bias_ref[head, span, 0:LANES] = found(place, head)
        return carry

    lax.fori_loop(0, TOK // 8, block, 0)

    def tail(step, carry):
        place = packed_ref[pl.ds(pl.multiple_of(step * 8, 8), 8), :]
        for head in range(HEADS):
            total = found(place, head)
            for k in range(4):
                span = pl.ds(pl.multiple_of(PADDED * k + step * 8, 8), 8)
                bias_ref[head, span, LANES : LANES + 32] = total[:, 32 * k : 32 * k + 32]
        return carry

    lax.fori_loop(0, PADDED // 8, tail, 0)


def remote(src, dst, send_sem, recv_sem, device):
    return pltpu.make_async_remote_copy(
        src_ref=src,
        dst_ref=dst,
        send_sem=send_sem,
        recv_sem=recv_sem,
        device_id=device,
        device_id_type=pl.DeviceIdType.MESH,
    )


def enter_kernel(
    lat_count,
    lon_count,
    mask_ref,
    fields_ref,
    cot_ref,
    table_ref,
    index_ref,
    q0,
    q1,
    q2,
    q3,
    bias_ref,
    place_ref,
    spread,
    held,
    leaving,
    landed,
    table,
    packed_ref,
    send_sem,
    recv_sem,
):
    lat, lon = lax.axis_index("lat"), lax.axis_index("lon")
    before_lat = (lat - 1 + lat_count) % lat_count
    before_lon = (lon - 1 + lon_count) % lon_count
    after_lat = (lat + 1) % lat_count
    after_lon = (lon + 1) % lon_count
    barrier = pltpu.get_barrier_semaphore()
    friends = [(before_lat, before_lon), (before_lat, lon), (lat, before_lon)]
    friends += [(after_lat, after_lon), (after_lat, lon), (lat, after_lon)]
    for friend in friends:
        pl.semaphore_signal(barrier, inc=1, device_id=friend, device_id_type=pl.DeviceIdType.MESH)
    pack(mask_ref, fields_ref, cot_ref, spread, held)
    for quad in range(3):
        leaving[quad] = held[quad].astype(LOW)
    q0[...] = held[3].astype(LOW)
    pl.semaphore_wait(barrier, len(friends))
    copies = [
        remote(leaving.at[i], landed.at[i], send_sem.at[i], recv_sem.at[i], friends[i]) for i in range(3)
    ]
    for each in copies:
        each.start()
    table[...] = jnp.zeros_like(table)
    for head in range(HEADS):
        table[head : head + 1, 0:NBIAS] = table_ref[head]
    lookup(table, index_ref, bias_ref, place_ref, packed_ref)
    for each in copies:
        each.wait()
    q3[...] = landed[0]
    q2[...] = landed[1]
    q1[...] = landed[2]


def window_kernel(
    place_ref,
    q0,
    q1,
    q2,
    q3,
    token_ref,
    gain_ref,
    qkv_w_ref,
    out_w_ref,
    bias_ref,
    y0,
    y1,
    y2,
    y3,
    wgrad_ref,
    vgrad_ref,
    pair_ref,
    qkv_s,
    gm_s,
    mixed_s,
    gqkv_s,
):
    scale = HEAD_DIM ** (-0.5)
    pieces = [ref[...].astype(WIDE) for ref in (q0, q1, q2, q3)]

    def gathered(lanes):
        return jnp.concatenate(
            [pieces[q][w * PADDED : w * PADDED + PADDED, lanes] for w in range(2) for q in range(4)], axis=0
        )

    spot = lax.broadcasted_iota(jnp.int32, (PADDED, 1), 0)
    marks = []
    for win in range(2):
        for quad in range(4):
            start = win * PADDED + PIECE
            first = pieces[quad][start : start + 1, 0:1]
            second = pieces[quad][start + 1 : start + 2, 0:1]
            marks.append(
                jnp.where(spot < 18, first, 0.0) + jnp.where((spot >= 18) & (spot < PIECE), second, 0.0)
            )
    masked = jnp.concatenate(marks, axis=0) > 0.5
    real = (lax.broadcasted_iota(jnp.int32, (2 * TOK, 1), 0) % PADDED) < PIECE
    gain = gain_ref[...].astype(WIDE)
    filled = jnp.where(masked, token_ref[...].astype(WIDE), gathered(slice(0, D)))
    filled = jnp.where(real, filled, 0.0)
    cot_wide = jnp.where(real, gathered(slice(D, 2 * D)), 0.0)
    cot = cot_wide.astype(LOW)
    center = filled - jnp.mean(filled, axis=-1, keepdims=True)
    inv_std = lax.rsqrt(jnp.mean(center * center, axis=-1, keepdims=True) + EPS)
    standard = center * inv_std
    normed = (standard * gain).astype(LOW)
    qkv_s[...] = nt(normed, qkv_w_ref[...]).astype(LOW)
    gm_s[...] = nn(cot, out_w_ref[...]).astype(LOW)

    edge = place_ref[0] == 1
    row_at = lax.broadcasted_iota(jnp.int32, (TOK, TOK), 0)
    col_at = lax.broadcasted_iota(jnp.int32, (TOK, TOK), 1)
    pad_col = (col_at % PADDED) >= PIECE
    lat_apart = ((row_at >= TOK // 2) != (col_at >= TOK // 2)) & edge
    level_apart = ((row_at % PADDED) >= 18) != ((col_at % PADDED) >= 18)
    fills = []
    for apart in (lat_apart, lat_apart | level_apart):
        fills.append(jnp.where(pad_col, NEVER, jnp.where(apart, BLOCKED, 0.0)))
    lane_head = lax.broadcasted_iota(jnp.int32, (TOK, LANES), 1) // HEAD_DIM

    for group in range(3):
        at = group * LANES
        parts = []
        for win in range(2):
            rows = slice(win * TOK, win * TOK + TOK)
            parts.append(
                (
                    qkv_s[rows, at : at + LANES],
                    qkv_s[rows, D + at : D + at + LANES],
                    qkv_s[rows, 2 * D + at : 2 * D + at + LANES],
                    gm_s[rows, at : at + LANES],
                )
            )
        sums = [[jnp.zeros((TOK, LANES), WIDE) for _ in range(4)] for _ in range(2)]
        for member in range(4):
            head = group * 4 + member
            mine = lane_head == member
            bias = bias_ref[head, :, 0:TOK]
            pair = jnp.zeros((TOK, TOK), WIDE)
            for win in range(2):
                query, key, value, gm = parts[win]
                none = jnp.zeros_like(query)
                query = jnp.where(mine, query, none)
                value_h = jnp.where(mine, value, none)
                gm_h = jnp.where(mine, gm, none)
                key_h = jnp.where(mine, key, none)
                scores = nt(query, key) * scale + bias
                scores = jnp.where(fills[win] == 0.0, scores, fills[win])
                exponent = jnp.exp(scores - jnp.max(scores, axis=-1, keepdims=True))
                prob = (exponent / jnp.sum(exponent, axis=-1, keepdims=True)).astype(LOW)
                grad_attn = nt(gm_h, value)
                prob_wide = prob.astype(WIDE)
                weighted = prob_wide * grad_attn
                grad_scores = weighted - prob_wide * jnp.sum(weighted, axis=-1, keepdims=True)
                pair = pair + grad_scores
                low = grad_scores.astype(LOW)
                sums[win][0] += nn(prob, value_h)
                sums[win][1] += nn(low, key_h)
                sums[win][2] += tn(low, query)
                sums[win][3] += tn(prob, gm_h)
            pair_ref[head] = pair
        for win in range(2):
            rows = slice(win * TOK, win * TOK + TOK)
            mixed, gq, gk, gv = sums[win]
            mixed_s[rows, at : at + LANES] = mixed.astype(LOW)
            gqkv_s[rows, at : at + LANES] = (gq * scale).astype(LOW)
            gqkv_s[rows, D + at : D + at + LANES] = (gk * scale).astype(LOW)
            gqkv_s[rows, 2 * D + at : 2 * D + at + LANES] = gv.astype(LOW)

    mixed = mixed_s[...]
    wgrad_ref[3 * D : 4 * D, :] = tn(cot, mixed).astype(wgrad_ref.dtype)
    for part in range(3):
        wgrad_ref[part * D : part * D + D, :] = tn(gqkv_s[:, part * D : part * D + D], normed).astype(
            wgrad_ref.dtype
        )
    branch = nt(mixed, out_w_ref[...]).astype(LOW).astype(WIDE)
    output = filled + branch
    grad_normed = nn(gqkv_s[...], qkv_w_ref[...]).astype(LOW).astype(WIDE)
    scaled = grad_normed * gain
    grad_filled = cot_wide + inv_std * (
        scaled
        - jnp.mean(scaled, axis=-1, keepdims=True)
        - standard * jnp.mean(scaled * standard, axis=-1, keepdims=True)
    )
    input_grad = jnp.where(masked, 0.0, grad_filled)
    vgrad_ref[...] = jnp.zeros((8, D), WIDE)
    vgrad_ref[0:1, :] = jnp.sum(grad_normed * standard, axis=0, keepdims=True)
    vgrad_ref[1:2, :] = jnp.sum(jnp.where(masked, grad_filled, 0.0), axis=0, keepdims=True)
    for quad, ref in enumerate((y0, y1, y2, y3)):
        for part, value in enumerate((output, input_grad)):
            both = [value[w * TOK + quad * PADDED : w * TOK + quad * PADDED + PADDED] for w in range(2)]
            ref[:, part * D : part * D + D] = jnp.concatenate(both, axis=0).astype(LOW)


def table_sums(pair_ref, place_ref, turned):
    for head in range(HEADS):
        turned[:, head, :] = pair_ref[head]
    turned[:, HEADS:ROWS, :] = jnp.zeros((TOK, ROWS - HEADS, TOK), WIDE)
    lane_at = lax.broadcasted_iota(jnp.int32, (LANES, TOK), 0)

    def step(block, total):
        for inner in range(8):
            row = block * 8 + inner
            place = place_ref[pl.ds(row, 1), 0:TOK]
            chunk = place >> 7
            hot = ((place & 127) == lane_at).astype(WIDE).astype(LOW)
            grad = turned[row]
            spread = jnp.concatenate([jnp.where(chunk == c, grad, 0.0) for c in range(CHUNKS)], axis=0)
            total = total + nt(spread.astype(LOW), hot)
        return total

    return lax.fori_loop(0, TOK // 8, step, jnp.zeros((CHUNKS * ROWS, LANES), WIDE))


def finish_kernel(
    lat_count,
    lon_count,
    y0,
    y1,
    y2,
    y3,
    terms_ref,
    vgrad_ref,
    pair_ref,
    place_ref,
    output_ref,
    grad_ref,
    rows_ref,
    table_ref,
    vector_ref,
    landed,
    held,
    spread,
    turned,
    pair_in,
    pair_sum,
    lon_in,
    lon_sum,
    lat_in,
    table_in,
    vec_in,
    vec_sum,
    vec_in_lat,
    quad_send,
    quad_recv,
    pair_send,
    pair_recv,
    lon_send,
    lon_recv,
    lat_send,
    lat_recv,
    table_send,
    table_recv,
    vec_send,
    vec_recv,
    vec_lat_send,
    vec_lat_recv,
):
    lat, lon = lax.axis_index("lat"), lax.axis_index("lon")
    half = lon_count // 2
    core, column = lon % 2, lon // 2

    def lat_at(step):
        return (lat + step + lat_count) % lat_count

    def lon_at(step):
        return (lon + step + lon_count) % lon_count

    barrier = pltpu.get_barrier_semaphore()
    friends = [(lat, lon_at(d)) for d in range(1, lon_count)]
    friends += [(lat_at(d), lon) for d in range(1, lat_count)]
    friends += [(lat_at(1), lon_at(1)), (lat_at(-1), lon_at(-1))]
    for friend in friends:
        pl.semaphore_signal(barrier, inc=1, device_id=friend, device_id_type=pl.DeviceIdType.MESH)
    pl.semaphore_wait(barrier, len(friends))

    pair_copy = remote(
        terms_ref.at[:, :, 1 - core], pair_in, pair_send, pair_recv, (lat, lon + 1 - 2 * core)
    )
    pair_copy.start()
    quads = [
        remote(y3, landed.at[0], quad_send.at[0], quad_recv.at[0], (lat_at(1), lon_at(1))),
        remote(y2, landed.at[1], quad_send.at[1], quad_recv.at[1], (lat_at(1), lon)),
        remote(y1, landed.at[2], quad_send.at[2], quad_recv.at[2], (lat, lon_at(1))),
    ]
    for each in quads:
        each.start()
    vec_in[lon] = vgrad_ref[...]
    vecs = []
    for d in range(1, lon_count):
        to = lon_at(d)
        vecs.append(remote(vgrad_ref, vec_in.at[lon], vec_send.at[to], vec_recv.at[lon], (lat, to)))
    for each in vecs:
        each.start()

    pair_copy.wait_recv()

    def add_pair(row, carry):
        for m in range(half):
            own = terms_ref[row, m, core].astype(WIDE)
            pair_sum[m, row] = (own + pair_in[row, m].astype(WIDE)).astype(LOW)
        return carry

    lax.fori_loop(0, lat_count, add_pair, 0)

    lon_copies = []
    for d in range(1, half):
        to = (column + d) % half
        lon_copies.append(
            remote(pair_sum.at[to], lon_in.at[column], lon_send.at[to], lon_recv.at[column], (lat, 2 * to + core))
        )
    for each in lon_copies:
        each.start()

    total = table_sums(pair_ref, place_ref, turned)
    for c in range(CHUNKS):
        table_in[lon, :, c * LANES : c * LANES + LANES] = total[c * ROWS : c * ROWS + ROWS].astype(LOW)
    tables = []
    for d in range(1, lon_count):
        to = lon_at(d)
        tables.append(remote(table_in.at[lon], table_in.at[lon], table_send.at[to], table_recv.at[lon], (lat, to)))
    for each in tables:
        each.start()

    for d in range(1, half):
        source = (column + d) % half
        remote(pair_sum.at[source], lon_in.at[source], lon_send.at[source], lon_recv.at[source], (lat, 2 * source + core)).wait_recv()

    def add_lon(row, carry):
        value = pair_sum[column, row].astype(WIDE)
        for d in range(1, half):
            value = value + lon_in[(column + d) % half, row].astype(WIDE)
        lon_sum[row] = value.astype(LOW)
        return carry

    lax.fori_loop(0, lat_count, add_lon, 0)

    lat_copies = []
    for d in range(1, lat_count):
        to = lat_at(d)
        lat_copies.append(remote(lon_sum.at[to], lat_in.at[lat], lat_send.at[to], lat_recv.at[lat], (to, lon)))
    for each in lat_copies:
        each.start()

    for d in range(1, lon_count):
        source = lon_at(d)
        remote(vgrad_ref, vec_in.at[source], vec_send.at[source], vec_recv.at[source], (lat, source)).wait_recv()
    vec = vec_in[0]
    for source in range(1, lon_count):
        vec = vec + vec_in[source]
    vec_sum[...] = vec
    vec_in_lat[lat] = vec
    vec_lats = []
    for d in range(1, lat_count):
        to = lat_at(d)
        vec_lats.append(remote(vec_sum, vec_in_lat.at[lat], vec_lat_send.at[to], vec_lat_recv.at[lat], (to, lon)))
    for each in vec_lats:
        each.start()

    for each in quads:
        each.wait_recv()
    for quad in range(3):
        held[quad] = landed[quad].astype(WIDE)
    held[3] = y0[...].astype(WIDE)
    unpack(held, spread, output_ref, grad_ref)

    for d in range(1, lon_count):
        source = lon_at(d)
        remote(
            table_in.at[source], table_in.at[source], table_send.at[source], table_recv.at[source], (lat, source)
        ).wait_recv()
    table = table_in[0].astype(WIDE)
    for source in range(1, lon_count):
        table = table + table_in[source].astype(WIDE)
    for head in range(HEADS):
        table_ref[head] = table[head : head + 1, 0:NBIAS]

    for d in range(1, lat_count):
        source = lat_at(d)
        remote(
            vec_sum, vec_in_lat.at[source], vec_lat_send.at[source], vec_lat_recv.at[source], (source, lon)
        ).wait_recv()
    vec = vec_in_lat[0]
    for source in range(1, lat_count):
        vec = vec + vec_in_lat[source]
    vector_ref[...] = vec[0:2]

    value = lon_sum[lat].astype(WIDE)
    for d in range(1, lat_count):
        source = lat_at(d)
        remote(lon_sum.at[source], lat_in.at[source], lat_send.at[source], lat_recv.at[source], (source, lon)).wait_recv()
        value = value + lat_in[source].astype(WIDE)
    rows_ref[...] = value

    for each in [pair_copy] + quads + vecs + lon_copies + tables + lat_copies + vec_lats:
        each.wait_send()


def struct(shape, dtype):
    return jax.ShapeDtypeStruct(shape, dtype)


def local(
    fields,
    cotangent,
    window_mask,
    mask_token,
    norm_gain,
    qkv_weight,
    out_weight,
    bias_table,
    bias_index,
):
    quad = struct((QUAD, 2 * D), LOW)
    lat_count, lon_count = lax.axis_size("lat"), lax.axis_size("lon")
    q0, q1, q2, q3, bias, place = pl.pallas_call(
        functools.partial(enter_kernel, lat_count, lon_count),
        out_shape=(quad,) * 4
        + (struct((HEADS, TOK, 2 * LANES), WIDE), struct((TOK, 2 * LANES), jnp.int32)),
        in_specs=[SMEM] + [VMEM] * 4,
        out_specs=(VMEM,) * 6,
        scratch_shapes=[
            pltpu.VMEM((2, 3, 288, LANES), WIDE),
            pltpu.VMEM((4, QUAD, 2 * D), WIDE),
            pltpu.VMEM((3, QUAD, 2 * D), LOW),
            pltpu.VMEM((3, QUAD, 2 * D), LOW),
            pltpu.VMEM((ROWS, CHUNKS * LANES), WIDE),
            pltpu.VMEM((PADDED, LANES), jnp.int32),
            pltpu.SemaphoreType.DMA((3,)),
            pltpu.SemaphoreType.DMA((3,)),
        ],
        compiler_params=pltpu.CompilerParams(
            collective_id=1, has_side_effects=True, vmem_limit_bytes=32 * 1024 * 1024
        ),
        name="enter",
    )(
        window_mask.transpose(1, 2, 0),
        fields.transpose(1, 2, 0, 3),
        cotangent.transpose(1, 2, 0, 3),
        bias_table.transpose(1, 0, 2),
        bias_index,
    )
    edge = (lax.axis_index("lat") == lax.axis_size("lat") - 1).astype(jnp.int32).reshape(1)
    y0, y1, y2, y3, wgrad, vgrad, pair = pl.pallas_call(
        window_kernel,
        out_shape=(quad,) * 4
        + (struct((4 * D, D), LOW), struct((8, D), WIDE), struct((HEADS, TOK, TOK), WIDE)),
        in_specs=[SMEM] + [VMEM] * 9,
        out_specs=(VMEM,) * 7,
        scratch_shapes=[
            pltpu.VMEM((2 * TOK, 3 * D), LOW),
            pltpu.VMEM((2 * TOK, D), LOW),
            pltpu.VMEM((2 * TOK, D), LOW),
            pltpu.VMEM((2 * TOK, 3 * D), LOW),
        ],
        compiler_params=PARAMS,
        name="windows",
    )(
        edge,
        q0,
        q1,
        q2,
        q3,
        mask_token.reshape(1, D),
        norm_gain.reshape(1, D),
        qkv_weight,
        out_weight,
        bias,
    )
    half = lon_count // 2
    share = 4 * D // (lat_count * lon_count)
    output, input_grad, weight_grads, table_grad, vector_grads = pl.pallas_call(
        functools.partial(finish_kernel, lat_count, lon_count),
        out_shape=(
            struct((6, 12, 4, D), LOW),
            struct((6, 12, 4, D), LOW),
            struct((share, D), WIDE),
            struct((HEADS, 1, NBIAS), WIDE),
            struct((2, D), WIDE),
        ),
        in_specs=[VMEM] * 8,
        out_specs=(VMEM,) * 5,
        scratch_shapes=[
            pltpu.VMEM((3, QUAD, 2 * D), LOW),
            pltpu.VMEM((4, QUAD, 2 * D), WIDE),
            pltpu.VMEM((2, 3, 288, LANES), WIDE),
            pltpu.VMEM((TOK, ROWS, TOK), WIDE),
            pltpu.VMEM((lat_count, half, share, D), LOW),
            pltpu.VMEM((half, lat_count, share, D), LOW),
            pltpu.VMEM((half, lat_count, share, D), LOW),
            pltpu.VMEM((lat_count, share, D), LOW),
            pltpu.VMEM((lat_count, share, D), LOW),
            pltpu.VMEM((lon_count, ROWS, CHUNKS * LANES), LOW),
            pltpu.VMEM((lon_count, 8, D), WIDE),
            pltpu.VMEM((8, D), WIDE),
            pltpu.VMEM((lat_count, 8, D), WIDE),
            pltpu.SemaphoreType.DMA((3,)),
            pltpu.SemaphoreType.DMA((3,)),
            pltpu.SemaphoreType.DMA,
            pltpu.SemaphoreType.DMA,
            pltpu.SemaphoreType.DMA((half,)),
            pltpu.SemaphoreType.DMA((half,)),
            pltpu.SemaphoreType.DMA((lat_count,)),
            pltpu.SemaphoreType.DMA((lat_count,)),
            pltpu.SemaphoreType.DMA((lon_count,)),
            pltpu.SemaphoreType.DMA((lon_count,)),
            pltpu.SemaphoreType.DMA((lon_count,)),
            pltpu.SemaphoreType.DMA((lon_count,)),
            pltpu.SemaphoreType.DMA((lat_count,)),
            pltpu.SemaphoreType.DMA((lat_count,)),
        ],
        compiler_params=pltpu.CompilerParams(
            collective_id=0, has_side_effects=True, vmem_limit_bytes=32 * 1024 * 1024
        ),
        name="finish",
    )(y0, y1, y2, y3, wgrad.reshape(lat_count, half, 2, share, D), vgrad, pair, place)
    output = output.transpose(2, 0, 1, 3)
    input_grad = input_grad.transpose(2, 0, 1, 3)
    table_grad = table_grad.transpose(1, 0, 2)
    return (output, input_grad, weight_grads, table_grad, vector_grads)


def solution(mesh):
    placed = (
        P(None, "lat", "lon", None),
        P(None, "lat", "lon", None),
        P(None, "lat", "lon"),
        P(),
        P(),
        P(),
        P(),
        P("lat", None, None),
        P(),
    )
    return jax.shard_map(
        local,
        mesh=mesh,
        in_specs=placed,
        out_specs=(
            P(None, "lat", "lon", None),
            P(None, "lat", "lon", None),
            P(("lat", "lon"), None),
            P("lat", None, None),
            P(),
        ),
        check_vma=False,
    )
```

```python
import functools

import jax
import jax.numpy as jnp
from jax import lax
from jax.experimental import pallas as pl
from jax.experimental.pallas import tpu as pltpu
from jax.sharding import PartitionSpec as P

D = 384
HEADS = 12
HEAD_DIM = 32
NBIAS = 759
EPS = 1e-05
BLOCKED = -10000.0
NEVER = -1e30

PIECE = 36
PADDED = 40
TOK = 4 * PADDED
QUAD = 2 * PADDED
CHUNKS = 6
LANES = 128
ROWS = 16

WIDE = jnp.float32
LOW = jnp.bfloat16
VMEM = pl.BlockSpec(memory_space=pltpu.VMEM)
SMEM = pl.BlockSpec(memory_space=pltpu.SMEM)
HBM = pl.BlockSpec(memory_space=pltpu.HBM)
LIMIT = 60 * 1024 * 1024
PARAMS = pltpu.CompilerParams(vmem_limit_bytes=64 * 1024 * 1024)


def nn(a, b):
    return lax.dot_general(a, b, (((1,), (0,)), ((), ())), preferred_element_type=WIDE)


def nt(a, b):
    return lax.dot_general(a, b, (((1,), (1,)), ((), ())), preferred_element_type=WIDE)


def tn(a, b):
    return lax.dot_general(a, b, (((0,), (0,)), ((), ())), preferred_element_type=WIDE)


def places():
    for level in range(4):
        shifted = (level - 1) % 4
        for row in range(6):
            yield level, row, row // 3, (shifted // 2) * PADDED + (shifted % 2) * 18 + (row % 3) * 6


def token_of(place):
    quad = place // PADDED
    within = place % PADDED
    level = within // 18
    row = (within % 18) // 6 + (quad // 2) * 3
    col = within % 6 + (quad % 2) * 6
    return jnp.where(within < PIECE, level * 72 + row * 12 + col, -1)


def pack(mask_ref, fields_ref, cot_ref, spread, held):
    for quad in range(4):
        for win in range(2):
            start = win * PADDED + PIECE - 4
            held[quad, start : start + 8, :] = jnp.zeros((8, 2 * D), WIDE)
    for part, ref in enumerate((fields_ref, cot_ref)):
        for row in range(6):
            for col in range(12):
                start = (row * 12 + col) * 4
                value = ref[row, col].astype(WIDE)
                for c in range(3):
                    spread[part, c, start : start + 4, :] = value[:, c * LANES : c * LANES + LANES]
        for level, row, half, start in places():
            for side in range(2):
                base = (row * 12 + side * 6) * 4 + level
                for c in range(3):
                    lanes = slice(part * D + c * LANES, part * D + c * LANES + LANES)
                    held[2 * half + side, start : start + 6, lanes] = spread[part, c, pl.ds(base, 6, stride=4), :]
    low = mask_ref[0, 0, 0].astype(WIDE)
    high = mask_ref[0, 0, 1].astype(WIDE)
    for quad in range(4):
        for win, (first, second) in enumerate(((low, high), (high, low))):
            start = win * PADDED + PIECE
            held[quad, start : start + 1, :] = jnp.full((1, 2 * D), first)
            held[quad, start + 1 : start + 2, :] = jnp.full((1, 2 * D), second)


def unpack(held, spread, output_ref, grad_ref):
    for part, ref in enumerate((output_ref, grad_ref)):
        for level, row, half, start in places():
            for side in range(2):
                base = (row * 12 + side * 6) * 4 + level
                for c in range(3):
                    lanes = slice(part * D + c * LANES, part * D + c * LANES + LANES)
                    spread[part, c, pl.ds(base, 6, stride=4), :] = held[2 * half + side, start : start + 6, lanes]
        for row in range(6):
            for col in range(12):
                start = (row * 12 + col) * 4
                value = [spread[part, c, start : start + 4, :] for c in range(3)]
                ref[row, col] = jnp.concatenate(value, axis=1).astype(LOW)


def lookup(table_ref, index_ref, bias_ref, place_ref, packed_ref):
    rows = lax.broadcasted_iota(jnp.int32, (TOK, 144), 0)
    pick_rows = (token_of(rows) == lax.broadcasted_iota(jnp.int32, (TOK, 144), 1)).astype(WIDE).astype(LOW)
    cols = lax.broadcasted_iota(jnp.int32, (2 * LANES, 144), 0)
    cols = jnp.where(cols < TOK, token_of(cols), -1)
    pick_cols = (cols == lax.broadcasted_iota(jnp.int32, (2 * LANES, 144), 1)).astype(WIDE).astype(LOW)
    index = index_ref[...]
    high = (index >> 7).astype(WIDE).astype(LOW)
    low = (index & 127).astype(WIDE).astype(LOW)
    high = nt(nn(pick_rows, high).astype(LOW), pick_cols).astype(jnp.int32)
    low = nt(nn(pick_rows, low).astype(LOW), pick_cols).astype(jnp.int32)
    place_ref[...] = high * LANES + low
    for k in range(4):
        packed_ref[:, 32 * k : 32 * k + 32] = place_ref[PADDED * k : PADDED * k + PADDED, LANES : LANES + 32]

    def found(place, head):
        chunk = place >> 7
        lane = place & 127
        total = jnp.zeros((8, LANES), WIDE)
        for c in range(CHUNKS):
            row = table_ref[head : head + 1, c * LANES : c * LANES + LANES]
            got = jnp.take_along_axis(jnp.broadcast_to(row, (8, LANES)), lane, axis=1)
            total = jnp.where(chunk == c, got, total)
        return total

    def block(step, carry):
        span = pl.ds(pl.multiple_of(step * 8, 8), 8)
        place = place_ref[span, 0:LANES]
        for head in range(HEADS):
            bias_ref[head, span, 0:LANES] = found(place, head)
        return carry

    lax.fori_loop(0, TOK // 8, block, 0)

    def tail(step, carry):
        place = packed_ref[pl.ds(pl.multiple_of(step * 8, 8), 8), :]
        for head in range(HEADS):
            total = found(place, head)
            for k in range(4):
                span = pl.ds(pl.multiple_of(PADDED * k + step * 8, 8), 8)
                bias_ref[head, span, LANES : LANES + 32] = total[:, 32 * k : 32 * k + 32]
        return carry

    lax.fori_loop(0, PADDED // 8, tail, 0)


def remote(src, dst, send_sem, recv_sem, device):
    return pltpu.make_async_remote_copy(
        src_ref=src,
        dst_ref=dst,
        send_sem=send_sem,
        recv_sem=recv_sem,
        device_id=device,
        device_id_type=pl.DeviceIdType.MESH,
    )


def enter(
    friends,
    loads,
    mask_ref,
    fields_ref,
    cot_ref,
    table_ref,
    index_ref,
    bias_ref,
    place_ref,
    spread,
    held,
    leaving,
    landed,
    table,
    packed_ref,
    send_sem,
    recv_sem,
    greeted,
):
    loads[0].wait()
    loads[1].wait()
    pack(mask_ref, fields_ref, cot_ref, spread, held)
    for quad in range(3):
        leaving[quad] = held[quad].astype(LOW)
    leaving[3] = held[3].astype(LOW)
    greeted()
    copies = [
        remote(leaving.at[i], landed.at[i], send_sem.at[i], recv_sem.at[i], friends[i]) for i in range(3)
    ]
    for each in copies:
        each.start()
    loads[2].wait()
    loads[3].wait()
    table[...] = jnp.zeros_like(table)
    for head in range(HEADS):
        table[head : head + 1, 0:NBIAS] = table_ref[head]
    lookup(table, index_ref, bias_ref, place_ref, packed_ref)
    for each in copies:
        each.wait_recv()
    return copies


def position(lat, lat_count):
    return (lat // 2 + lat) % 2 * (lat_count // 2) + lat // 2


def attend(
    lat_count,
    lon_count,
    edge,
    q0,
    q1,
    q2,
    q3,
    token_ref,
    gain_ref,
    qkv_w_ref,
    out_w_ref,
    bias_ref,
    y0,
    y1,
    y2,
    y3,
    wgrad_ref,
    vgrad_ref,
    pair_ref,
    qkv_s,
    gm_s,
    mixed_s,
    gqkv_s,
):
    scale = HEAD_DIM ** (-0.5)
    pieces = [ref[...].astype(WIDE) for ref in (q0, q1, q2, q3)]

    def gathered(lanes):
        return jnp.concatenate(
            [pieces[q][w * PADDED : w * PADDED + PADDED, lanes] for w in range(2) for q in range(4)], axis=0
        )

    spot = lax.broadcasted_iota(jnp.int32, (PADDED, 1), 0)
    marks = []
    for win in range(2):
        for quad in range(4):
            start = win * PADDED + PIECE
            first = pieces[quad][start : start + 1, 0:1]
            second = pieces[quad][start + 1 : start + 2, 0:1]
            marks.append(
                jnp.where(spot < 18, first, 0.0) + jnp.where((spot >= 18) & (spot < PIECE), second, 0.0)
            )
    masked = jnp.concatenate(marks, axis=0) > 0.5
    real = (lax.broadcasted_iota(jnp.int32, (2 * TOK, 1), 0) % PADDED) < PIECE
    gain = gain_ref[...].astype(WIDE).reshape(1, D)
    filled = jnp.where(masked, token_ref[...].astype(WIDE).reshape(1, D), gathered(slice(0, D)))
    filled = jnp.where(real, filled, 0.0)
    cot_wide = jnp.where(real, gathered(slice(D, 2 * D)), 0.0)
    cot = cot_wide.astype(LOW)
    center = filled - jnp.mean(filled, axis=-1, keepdims=True)
    inv_std = lax.rsqrt(jnp.mean(center * center, axis=-1, keepdims=True) + EPS)
    standard = center * inv_std
    normed = (standard * gain).astype(LOW)
    qkv_s[...] = nt(normed, qkv_w_ref[...]).astype(LOW)
    gm_s[...] = nn(cot, out_w_ref[...]).astype(LOW)

    row_at = lax.broadcasted_iota(jnp.int32, (TOK, TOK), 0)
    col_at = lax.broadcasted_iota(jnp.int32, (TOK, TOK), 1)
    pad_col = (col_at % PADDED) >= PIECE
    lat_apart = ((row_at >= TOK // 2) != (col_at >= TOK // 2)) & edge
    level_apart = ((row_at % PADDED) >= 18) != ((col_at % PADDED) >= 18)
    fills = []
    for apart in (lat_apart, lat_apart | level_apart):
        fills.append(jnp.where(pad_col, NEVER, jnp.where(apart, BLOCKED, 0.0)))
    lane_head = lax.broadcasted_iota(jnp.int32, (TOK, LANES), 1) // HEAD_DIM

    for group in range(3):
        at = group * LANES
        parts = []
        for win in range(2):
            rows = slice(win * TOK, win * TOK + TOK)
            parts.append(
                (
                    qkv_s[rows, at : at + LANES],
                    qkv_s[rows, D + at : D + at + LANES],
                    qkv_s[rows, 2 * D + at : 2 * D + at + LANES],
                    gm_s[rows, at : at + LANES],
                )
            )
        sums = [[jnp.zeros((TOK, LANES), WIDE) for _ in range(4)] for _ in range(2)]
        for member in range(4):
            head = group * 4 + member
            mine = lane_head == member
            bias = bias_ref[head, :, 0:TOK]
            pair = jnp.zeros((TOK, TOK), WIDE)
            for win in range(2):
                query, key, value, gm = parts[win]
                none = jnp.zeros_like(query)
                query = jnp.where(mine, query, none)
                value_h = jnp.where(mine, value, none)
                gm_h = jnp.where(mine, gm, none)
                key_h = jnp.where(mine, key, none)
                scores = nt(query, key) * scale + bias
                scores = jnp.where(fills[win] == 0.0, scores, fills[win])
                exponent = jnp.exp(scores - jnp.max(scores, axis=-1, keepdims=True))
                prob = (exponent / jnp.sum(exponent, axis=-1, keepdims=True)).astype(LOW)
                grad_attn = nt(gm_h, value)
                prob_wide = prob.astype(WIDE)
                weighted = prob_wide * grad_attn
                grad_scores = weighted - prob_wide * jnp.sum(weighted, axis=-1, keepdims=True)
                pair = pair + grad_scores
                low = grad_scores.astype(LOW)
                sums[win][0] += nn(prob, value_h)
                sums[win][1] += nn(low, key_h)
                sums[win][2] += tn(low, query)
                sums[win][3] += tn(prob, gm_h)
            pair_ref[head] = pair
        for win in range(2):
            rows = slice(win * TOK, win * TOK + TOK)
            mixed, gq, gk, gv = sums[win]
            mixed_s[rows, at : at + LANES] = mixed.astype(LOW)
            gqkv_s[rows, at : at + LANES] = (gq * scale).astype(LOW)
            gqkv_s[rows, D + at : D + at + LANES] = (gk * scale).astype(LOW)
            gqkv_s[rows, 2 * D + at : 2 * D + at + LANES] = gv.astype(LOW)

    mixed = mixed_s[...]
    band = 4 * D // lat_count
    share = band // lon_count
    for part in range(4):
        value = tn(cot, mixed) if part == 3 else tn(gqkv_s[:, part * D : part * D + D], normed)
        for i in range(lat_count // 4):
            at = position(part * (lat_count // 4) + i, lat_count)
            for n in range(lon_count):
                first = i * band + n * share
                wgrad_ref[at, n // 2, n % 2] = value[first : first + share].astype(LOW)
    branch = nt(mixed, out_w_ref[...]).astype(LOW).astype(WIDE)
    output = filled + branch
    grad_normed = nn(gqkv_s[...], qkv_w_ref[...]).astype(LOW).astype(WIDE)
    scaled = grad_normed * gain
    grad_filled = cot_wide + inv_std * (
        scaled
        - jnp.mean(scaled, axis=-1, keepdims=True)
        - standard * jnp.mean(scaled * standard, axis=-1, keepdims=True)
    )
    input_grad = jnp.where(masked, 0.0, grad_filled)
    vgrad_ref[...] = jnp.zeros((8, D), WIDE)
    vgrad_ref[0:1, :] = jnp.sum(grad_normed * standard, axis=0, keepdims=True)
    vgrad_ref[1:2, :] = jnp.sum(jnp.where(masked, grad_filled, 0.0), axis=0, keepdims=True)
    for quad, ref in enumerate((y0, y1, y2, y3)):
        for part, value in enumerate((output, input_grad)):
            both = [value[w * TOK + quad * PADDED : w * TOK + quad * PADDED + PADDED] for w in range(2)]
            ref[:, part * D : part * D + D] = jnp.concatenate(both, axis=0).astype(LOW)


def turn(pair_ref, turned):
    for head in range(HEADS):
        turned[:, head, :] = pair_ref[head]
    turned[:, HEADS:ROWS, :] = jnp.zeros((TOK, ROWS - HEADS, TOK), WIDE)


def table_sums(first, last, total, place_ref, turned):
    lane_at = lax.broadcasted_iota(jnp.int32, (LANES, TOK), 0)

    def step(block, total):
        for inner in range(8):
            row = block * 8 + inner
            place = place_ref[pl.ds(row, 1), 0:TOK]
            chunk = place >> 7
            hot = ((place & 127) == lane_at).astype(WIDE).astype(LOW)
            grad = turned[row]
            spread = jnp.concatenate([jnp.where(chunk == c, grad, 0.0) for c in range(CHUNKS)], axis=0)
            total = total + nt(spread.astype(LOW), hot)
        return total

    return lax.fori_loop(first, last, step, total)


def block_kernel(
    lat_count,
    lon_count,
    mask_ref,
    fields_hbm,
    cot_hbm,
    table_hbm,
    index_hbm,
    qkv_w_hbm,
    out_w_hbm,
    token_ref,
    gain_ref,
    output_ref,
    grad_ref,
    rows_ref,
    table_ref,
    vector_ref,
    fields_v,
    cot_v,
    table_v,
    index_v,
    qkv_w_v,
    out_w_v,
    load_sem,
    spread,
    held,
    leaving,
    arrived,
    padded_table,
    packed_ref,
    in_send,
    in_recv,
    bias_ref,
    place_ref,
    ys,
    terms_ref,
    vgrad_ref,
    pair_ref,
    qkv_s,
    gm_s,
    mixed_s,
    gqkv_s,
    landed,
    turned,
    pair_in,
    pair_sum,
    lon_in,
    lon_sum,
    lat_in,
    table_in,
    vec_in,
    vec_sum,
    vec_in_lat,
    quad_send,
    quad_recv,
    pair_send,
    pair_recv,
    lon_send,
    lon_recv,
    lat_send,
    lat_recv,
    table_send,
    table_recv,
    vec_send,
    vec_recv,
    vec_lat_send,
    vec_lat_recv,
):
    lat, lon = lax.axis_index("lat"), lax.axis_index("lon")
    half = lon_count // 2
    core, column = lon % 2, lon // 2

    def lat_at(step):
        return (lat + step + lat_count) % lat_count

    def lon_at(step):
        return (lon + step + lon_count) % lon_count

    barrier = pltpu.get_barrier_semaphore()
    friends = [(lat, lon_at(d)) for d in range(1, lon_count)]
    friends += [(lat_at(d), lon) for d in range(1, lat_count)]
    friends += [(lat_at(1), lon_at(1)), (lat_at(-1), lon_at(-1))]
    for friend in friends:
        pl.semaphore_signal(barrier, inc=1, device_id=friend, device_id_type=pl.DeviceIdType.MESH)
    pairs = (
        (fields_hbm, fields_v),
        (cot_hbm, cot_v),
        (table_hbm, table_v),
        (index_hbm, index_v),
        (qkv_w_hbm, qkv_w_v),
        (out_w_hbm, out_w_v),
    )
    loads = [pltpu.make_async_copy(src, dst, load_sem.at[i]) for i, (src, dst) in enumerate(pairs)]
    for each in loads:
        each.start()

    in_copies = enter(
        [(lat_at(-1), lon_at(-1)), (lat_at(-1), lon), (lat, lon_at(-1))],
        loads,
        mask_ref,
        fields_v,
        cot_v,
        table_v,
        index_v,
        bias_ref,
        place_ref,
        spread,
        held,
        leaving,
        arrived,
        padded_table,
        packed_ref,
        in_send,
        in_recv,
        lambda: pl.semaphore_wait(barrier, len(friends)),
    )
    loads[4].wait()
    loads[5].wait()
    y0, y1, y2, y3 = (ys.at[i] for i in range(4))
    attend(
        lat_count,
        lon_count,
        lat == lat_count - 1,
        leaving.at[3],
        arrived.at[2],
        arrived.at[1],
        arrived.at[0],
        token_ref,
        gain_ref,
        qkv_w_v,
        out_w_v,
        bias_ref,
        y0,
        y1,
        y2,
        y3,
        terms_ref,
        vgrad_ref,
        pair_ref,
        qkv_s,
        gm_s,
        mixed_s,
        gqkv_s,
    )

    members = lat_count // 2
    mine = (lat // 2 + lat) % 2
    halves = (1 - mine, mine)
    spans = [pl.ds(h * members, members) for h in halves]

    pair_copies = [
        remote(
            terms_ref.at[span, :, 1 - core],
            pair_in.at[span],
            pair_send.at[i],
            pair_recv.at[i],
            (lat, lon + 1 - 2 * core),
        )
        for i, span in enumerate(spans)
    ]
    for each in pair_copies:
        each.start()
    quads = [
        remote(y3, landed.at[0], quad_send.at[0], quad_recv.at[0], (lat_at(1), lon_at(1))),
        remote(y2, landed.at[1], quad_send.at[1], quad_recv.at[1], (lat_at(1), lon)),
        remote(y1, landed.at[2], quad_send.at[2], quad_recv.at[2], (lat, lon_at(1))),
    ]
    for each in quads:
        each.start()
    vec_in[lon] = vgrad_ref[...]
    vecs = []
    for d in range(1, lon_count):
        to = lon_at(d)
        vecs.append(remote(vgrad_ref, vec_in.at[lon], vec_send.at[to], vec_recv.at[lon], (lat, to)))
    for each in vecs:
        each.start()

    turn(pair_ref, turned)
    lon_copies = []
    for i in range(2):
        pair_copies[i].wait_recv()

        def add_pair(step, carry, base=halves[i] * members):
            row = base + step
            for m in range(half):
                own = terms_ref[row, m, core].astype(WIDE)
                pair_sum[m, row] = (own + pair_in[row, m].astype(WIDE)).astype(LOW)
            return carry

        lax.fori_loop(0, members, add_pair, 0)
        for d in range(1, half):
            to = (column + d) % half
            each = remote(
                pair_sum.at[to, spans[i]],
                lon_in.at[column, spans[i]],
                lon_send.at[i, to],
                lon_recv.at[i, column],
                (lat, 2 * to + core),
            )
            each.start()
            lon_copies.append(each)

    total = jnp.zeros((CHUNKS * ROWS, LANES), WIDE)
    lat_copies = []
    for i in range(2):
        total = table_sums(8 * i, 8 * i + 8, total, place_ref, turned)
        for d in range(1, half):
            source = (column + d) % half
            remote(
                pair_sum.at[source, spans[i]],
                lon_in.at[source, spans[i]],
                lon_send.at[i, source],
                lon_recv.at[i, source],
                (lat, 2 * source + core),
            ).wait_recv()

        def add_lon(step, carry, base=halves[i] * members):
            row = base + step
            value = pair_sum[column, row].astype(WIDE)
            for d in range(1, half):
                value = value + lon_in[(column + d) % half, row].astype(WIDE)
            lon_sum[row] = value.astype(LOW)
            return carry

        lax.fori_loop(0, members, add_lon, 0)
        for d in range(i, members):
            group = (lat // 2 + d) % members
            to = 2 * group + (group + halves[i]) % 2
            each = remote(
                lon_sum.at[halves[i] * members + group], lat_in.at[lat], lat_send.at[to], lat_recv.at[lat], (to, lon)
            )
            each.start()
            lat_copies.append(each)

    total = table_sums(16, TOK // 8, total, place_ref, turned)
    for c in range(CHUNKS):
        table_in[lon, :, c * LANES : c * LANES + LANES] = total[c * ROWS : c * ROWS + ROWS].astype(LOW)
    tables = []
    for d in range(1, lon_count):
        to = lon_at(d)
        tables.append(remote(table_in.at[lon], table_in.at[lon], table_send.at[to], table_recv.at[lon], (lat, to)))
    for each in tables:
        each.start()

    for d in range(1, lon_count):
        source = lon_at(d)
        remote(vgrad_ref, vec_in.at[source], vec_send.at[source], vec_recv.at[source], (lat, source)).wait_recv()
    vec = vec_in[0]
    for source in range(1, lon_count):
        vec = vec + vec_in[source]
    vec_sum[...] = vec
    vec_in_lat[lat] = vec
    vec_lats = []
    for d in range(1, lat_count):
        to = lat_at(d)
        vec_lats.append(remote(vec_sum, vec_in_lat.at[lat], vec_lat_send.at[to], vec_lat_recv.at[lat], (to, lon)))
    for each in vec_lats:
        each.start()

    for each in quads:
        each.wait_recv()
    for quad in range(3):
        held[quad] = landed[quad].astype(WIDE)
    held[3] = y0[...].astype(WIDE)
    unpack(held, spread, output_ref, grad_ref)

    for d in range(1, lon_count):
        source = lon_at(d)
        remote(
            table_in.at[source], table_in.at[source], table_send.at[source], table_recv.at[source], (lat, source)
        ).wait_recv()
    table = table_in[0].astype(WIDE)
    for source in range(1, lon_count):
        table = table + table_in[source].astype(WIDE)
    for head in range(HEADS):
        table_ref[head] = table[head : head + 1, 0:NBIAS]

    for d in range(1, lat_count):
        source = lat_at(d)
        remote(
            vec_sum, vec_in_lat.at[source], vec_lat_send.at[source], vec_lat_recv.at[source], (source, lon)
        ).wait_recv()
    vec = vec_in_lat[0]
    for source in range(1, lat_count):
        vec = vec + vec_in_lat[source]
    vector_ref[...] = vec[0:2]

    value = lon_sum[position(lat, lat_count)].astype(WIDE)
    for d in range(1, lat_count):
        source = lat_at(d)
        remote(lon_sum.at[0], lat_in.at[source], lat_send.at[source], lat_recv.at[source], (source, lon)).wait_recv()
        value = value + lat_in[source].astype(WIDE)
    rows_ref[...] = value

    for each in in_copies + pair_copies + quads + vecs + lon_copies + tables + lat_copies + vec_lats:
        each.wait_send()


def write_kernel(*refs):
    sems = refs[10]
    copies = [pltpu.make_async_copy(refs[i], refs[5 + i], sems.at[i]) for i in range(5)]
    for each in copies:
        each.start()
    for each in copies:
        each.wait()


def struct(shape, dtype):
    return jax.ShapeDtypeStruct(shape, dtype)


def local(
    fields,
    cotangent,
    window_mask,
    mask_token,
    norm_gain,
    qkv_weight,
    out_weight,
    bias_table,
    bias_index,
):
    lat_count, lon_count = lax.axis_size("lat"), lax.axis_size("lon")
    half = lon_count // 2
    share = 4 * D // (lat_count * lon_count)

    def low(*shape):
        return pltpu.VMEM(shape, LOW)

    def wide(*shape):
        return pltpu.VMEM(shape, WIDE)

    def sems(*shape):
        return [pltpu.SemaphoreType.DMA(shape)] * 2

    output, input_grad, weight_grads, table_grad, vector_grads = pl.pallas_call(
        functools.partial(block_kernel, lat_count, lon_count),
        out_shape=(
            struct((6, 12, 4, D), LOW),
            struct((6, 12, 4, D), LOW),
            struct((share, D), WIDE),
            struct((HEADS, 1, NBIAS), WIDE),
            struct((2, D), WIDE),
        ),
        in_specs=[SMEM] + [HBM] * 6 + [VMEM] * 2,
        out_specs=(VMEM,) * 5,
        scratch_shapes=[
            low(6, 12, 4, D),
            low(6, 12, 4, D),
            wide(HEADS, 1, NBIAS),
            pltpu.VMEM((144, 144), jnp.int32),
            low(3 * D, D),
            low(D, D),
            pltpu.SemaphoreType.DMA((6,)),
            wide(2, 3, 288, LANES),
            wide(4, QUAD, 2 * D),
            low(4, QUAD, 2 * D),
            low(3, QUAD, 2 * D),
            wide(ROWS, CHUNKS * LANES),
            pltpu.VMEM((PADDED, LANES), jnp.int32),
            *sems(3),
            wide(HEADS, TOK, 2 * LANES),
            pltpu.VMEM((TOK, 2 * LANES), jnp.int32),
            low(4, QUAD, 2 * D),
            low(lat_count, half, 2, share, D),
            wide(8, D),
            wide(HEADS, TOK, TOK),
            low(2 * TOK, 3 * D),
            low(2 * TOK, D),
            low(2 * TOK, D),
            low(2 * TOK, 3 * D),
            low(3, QUAD, 2 * D),
            wide(TOK, ROWS, TOK),
            low(lat_count, half, share, D),
            low(half, lat_count, share, D),
            low(half, lat_count, share, D),
            low(lat_count, share, D),
            low(lat_count, share, D),
            low(lon_count, ROWS, CHUNKS * LANES),
            wide(lon_count, 8, D),
            wide(8, D),
            wide(lat_count, 8, D),
            *sems(3),
            *sems(2),
            *sems(2, half),
            *sems(lat_count),
            *sems(lon_count),
            *sems(lon_count),
            *sems(lat_count),
        ],
        compiler_params=pltpu.CompilerParams(
            collective_id=0, has_side_effects=True, vmem_limit_bytes=LIMIT
        ),
        name="block",
    )(
        window_mask.transpose(1, 2, 0),
        fields.transpose(1, 2, 0, 3),
        cotangent.transpose(1, 2, 0, 3),
        bias_table.transpose(1, 0, 2),
        bias_index,
        qkv_weight,
        out_weight,
        mask_token,
        norm_gain,
    )
    results = (output, input_grad, weight_grads, table_grad, vector_grads)
    output, input_grad, weight_grads, table_grad, vector_grads = pl.pallas_call(
        write_kernel,
        out_shape=tuple(struct(each.shape, each.dtype) for each in results),
        in_specs=[HBM] * 5,
        out_specs=(HBM,) * 5,
        scratch_shapes=[pltpu.SemaphoreType.DMA((5,))],
        compiler_params=PARAMS,
        name="write",
    )(*results)
    output = output.transpose(2, 0, 1, 3)
    input_grad = input_grad.transpose(2, 0, 1, 3)
    table_grad = table_grad.transpose(1, 0, 2)
    return (output, input_grad, weight_grads, table_grad, vector_grads)


def solution(mesh):
    placed = (
        P(None, "lat", "lon", None),
        P(None, "lat", "lon", None),
        P(None, "lat", "lon"),
        P(),
        P(),
        P(),
        P(),
        P("lat", None, None),
        P(),
    )
    return jax.shard_map(
        local,
        mesh=mesh,
        in_specs=placed,
        out_specs=(
            P(None, "lat", "lon", None),
            P(None, "lat", "lon", None),
            P(("lat", "lon"), None),
            P("lat", None, None),
            P(),
        ),
        check_vma=False,
    )
```

```python
import functools

import jax
import jax.numpy as jnp
from jax import lax
from jax.experimental import pallas as pl
from jax.experimental.pallas import tpu as pltpu
from jax.sharding import PartitionSpec as P

D = 384
HEADS = 12
HEAD_DIM = 32
NBIAS = 759
EPS = 1e-05
BLOCKED = -10000.0
NEVER = -1e30

PIECE = 36
PADDED = 40
TOK = 4 * PADDED
QUAD = 2 * PADDED
CHUNKS = 6
LANES = 128
ROWS = 16

WIDE = jnp.float32
LOW = jnp.bfloat16
VMEM = pl.BlockSpec(memory_space=pltpu.VMEM)
SMEM = pl.BlockSpec(memory_space=pltpu.SMEM)
HBM = pl.BlockSpec(memory_space=pltpu.HBM)
LIMIT = 60 * 1024 * 1024
PARAMS = pltpu.CompilerParams(vmem_limit_bytes=64 * 1024 * 1024)


def nn(a, b):
    return lax.dot_general(a, b, (((1,), (0,)), ((), ())), preferred_element_type=WIDE)


def nt(a, b):
    return lax.dot_general(a, b, (((1,), (1,)), ((), ())), preferred_element_type=WIDE)


def tn(a, b):
    return lax.dot_general(a, b, (((0,), (0,)), ((), ())), preferred_element_type=WIDE)


def places():
    for level in range(4):
        shifted = (level - 1) % 4
        for row in range(6):
            yield level, row, row // 3, (shifted // 2) * PADDED + (shifted % 2) * 18 + (row % 3) * 6


def token_of(place):
    quad = place // PADDED
    within = place % PADDED
    level = within // 18
    row = (within % 18) // 6 + (quad // 2) * 3
    col = within % 6 + (quad % 2) * 6
    return jnp.where(within < PIECE, level * 72 + row * 12 + col, -1)


def pack(mask_ref, fields_ref, cot_ref, spread, held):
    for quad in range(4):
        for win in range(2):
            start = win * PADDED + PIECE - 4
            held[quad, start : start + 8, :] = jnp.zeros((8, 2 * D), WIDE)
    for part, ref in enumerate((fields_ref, cot_ref)):
        for row in range(6):
            for col in range(12):
                start = (row * 12 + col) * 4
                value = ref[row, col].astype(WIDE)
                for c in range(3):
                    spread[part, c, start : start + 4, :] = value[:, c * LANES : c * LANES + LANES]
        for level, row, half, start in places():
            for side in range(2):
                base = (row * 12 + side * 6) * 4 + level
                for c in range(3):
                    lanes = slice(part * D + c * LANES, part * D + c * LANES + LANES)
                    held[2 * half + side, start : start + 6, lanes] = spread[part, c, pl.ds(base, 6, stride=4), :]
    low = mask_ref[0, 0, 0].astype(WIDE)
    high = mask_ref[0, 0, 1].astype(WIDE)
    for quad in range(4):
        for win, (first, second) in enumerate(((low, high), (high, low))):
            start = win * PADDED + PIECE
            held[quad, start : start + 1, :] = jnp.full((1, 2 * D), first)
            held[quad, start + 1 : start + 2, :] = jnp.full((1, 2 * D), second)


def unpack(held, spread, output_ref, grad_ref):
    for part, ref in enumerate((output_ref, grad_ref)):
        for level, row, half, start in places():
            for side in range(2):
                base = (row * 12 + side * 6) * 4 + level
                for c in range(3):
                    lanes = slice(part * D + c * LANES, part * D + c * LANES + LANES)
                    spread[part, c, pl.ds(base, 6, stride=4), :] = held[2 * half + side, start : start + 6, lanes]
        for row in range(6):
            for col in range(12):
                start = (row * 12 + col) * 4
                value = [spread[part, c, start : start + 4, :] for c in range(3)]
                ref[row, col] = jnp.concatenate(value, axis=1).astype(LOW)


def lookup(table_ref, index_ref, bias_ref, place_ref, packed_ref):
    rows = lax.broadcasted_iota(jnp.int32, (TOK, 144), 0)
    pick_rows = (token_of(rows) == lax.broadcasted_iota(jnp.int32, (TOK, 144), 1)).astype(WIDE).astype(LOW)
    cols = lax.broadcasted_iota(jnp.int32, (2 * LANES, 144), 0)
    cols = jnp.where(cols < TOK, token_of(cols), -1)
    pick_cols = (cols == lax.broadcasted_iota(jnp.int32, (2 * LANES, 144), 1)).astype(WIDE).astype(LOW)
    index = index_ref[...]
    high = (index >> 7).astype(WIDE).astype(LOW)
    low = (index & 127).astype(WIDE).astype(LOW)
    high = nt(nn(pick_rows, high).astype(LOW), pick_cols).astype(jnp.int32)
    low = nt(nn(pick_rows, low).astype(LOW), pick_cols).astype(jnp.int32)
    place_ref[...] = high * LANES + low
    for k in range(4):
        packed_ref[:, 32 * k : 32 * k + 32] = place_ref[PADDED * k : PADDED * k + PADDED, LANES : LANES + 32]

    def found(place, head):
        chunk = place >> 7
        lane = place & 127
        total = jnp.zeros((8, LANES), WIDE)
        for c in range(CHUNKS):
            row = table_ref[head : head + 1, c * LANES : c * LANES + LANES]
            got = jnp.take_along_axis(jnp.broadcast_to(row, (8, LANES)), lane, axis=1)
            total = jnp.where(chunk == c, got, total)
        return total

    def block(step, carry):
        span = pl.ds(pl.multiple_of(step * 8, 8), 8)
        place = place_ref[span, 0:LANES]
        for head in range(HEADS):
            bias_ref[head, span, 0:LANES] = found(place, head)
        return carry

    lax.fori_loop(0, TOK // 8, block, 0)

    def tail(step, carry):
        place = packed_ref[pl.ds(pl.multiple_of(step * 8, 8), 8), :]
        for head in range(HEADS):
            total = found(place, head)
            for k in range(4):
                span = pl.ds(pl.multiple_of(PADDED * k + step * 8, 8), 8)
                bias_ref[head, span, LANES : LANES + 32] = total[:, 32 * k : 32 * k + 32]
        return carry

    lax.fori_loop(0, PADDED // 8, tail, 0)


def remote(src, dst, send_sem, recv_sem, device):
    return pltpu.make_async_remote_copy(
        src_ref=src,
        dst_ref=dst,
        send_sem=send_sem,
        recv_sem=recv_sem,
        device_id=device,
        device_id_type=pl.DeviceIdType.MESH,
    )


def enter(
    friends,
    loads,
    mask_ref,
    fields_ref,
    cot_ref,
    table_ref,
    index_ref,
    bias_ref,
    place_ref,
    spread,
    held,
    leaving,
    landed,
    table,
    packed_ref,
    send_sem,
    recv_sem,
    greeted,
):
    loads[0].wait()
    loads[1].wait()
    pack(mask_ref, fields_ref, cot_ref, spread, held)
    for quad in range(3):
        leaving[quad] = held[quad].astype(LOW)
    leaving[3] = held[3].astype(LOW)
    greeted()
    copies = [
        remote(leaving.at[i], landed.at[i], send_sem.at[i], recv_sem.at[i], friends[i]) for i in range(3)
    ]
    for each in copies:
        each.start()
    loads[2].wait()
    loads[3].wait()
    table[...] = jnp.zeros_like(table)
    for head in range(HEADS):
        table[head : head + 1, 0:NBIAS] = table_ref[head]
    lookup(table, index_ref, bias_ref, place_ref, packed_ref)
    for each in copies:
        each.wait_recv()
    return copies


def position(lat, lat_count):
    return (lat // 2 + lat) % 2 * (lat_count // 2) + lat // 2


def attend(
    lat_count,
    lon_count,
    edge,
    q0,
    q1,
    q2,
    q3,
    token_ref,
    gain_ref,
    qkv_w_ref,
    out_w_ref,
    bias_ref,
    y0,
    y1,
    y2,
    y3,
    wgrad_ref,
    vgrad_ref,
    pair_ref,
    qkv_s,
    gm_s,
    mixed_s,
    gqkv_s,
):
    scale = HEAD_DIM ** (-0.5)
    pieces = [ref[...].astype(WIDE) for ref in (q0, q1, q2, q3)]

    def gathered(lanes):
        return jnp.concatenate(
            [pieces[q][w * PADDED : w * PADDED + PADDED, lanes] for w in range(2) for q in range(4)], axis=0
        )

    spot = lax.broadcasted_iota(jnp.int32, (PADDED, 1), 0)
    marks = []
    for win in range(2):
        for quad in range(4):
            start = win * PADDED + PIECE
            first = pieces[quad][start : start + 1, 0:1]
            second = pieces[quad][start + 1 : start + 2, 0:1]
            marks.append(
                jnp.where(spot < 18, first, 0.0) + jnp.where((spot >= 18) & (spot < PIECE), second, 0.0)
            )
    masked = jnp.concatenate(marks, axis=0) > 0.5
    real = (lax.broadcasted_iota(jnp.int32, (2 * TOK, 1), 0) % PADDED) < PIECE
    gain = gain_ref[...].astype(WIDE).reshape(1, D)
    filled = jnp.where(masked, token_ref[...].astype(WIDE).reshape(1, D), gathered(slice(0, D)))
    filled = jnp.where(real, filled, 0.0)
    cot_wide = jnp.where(real, gathered(slice(D, 2 * D)), 0.0)
    cot = cot_wide.astype(LOW)
    center = filled - jnp.mean(filled, axis=-1, keepdims=True)
    inv_std = lax.rsqrt(jnp.mean(center * center, axis=-1, keepdims=True) + EPS)
    standard = center * inv_std
    normed = (standard * gain).astype(LOW)
    qkv_s[...] = nt(normed, qkv_w_ref[...]).astype(LOW)
    gm_s[...] = nn(cot, out_w_ref[...]).astype(LOW)

    row_at = lax.broadcasted_iota(jnp.int32, (TOK, TOK), 0)
    col_at = lax.broadcasted_iota(jnp.int32, (TOK, TOK), 1)
    pad_col = (col_at % PADDED) >= PIECE
    lat_apart = ((row_at >= TOK // 2) != (col_at >= TOK // 2)) & edge
    level_apart = ((row_at % PADDED) >= 18) != ((col_at % PADDED) >= 18)
    fills = []
    for apart in (lat_apart, lat_apart | level_apart):
        fills.append(jnp.where(pad_col, NEVER, jnp.where(apart, BLOCKED, 0.0)))
    lane_head = lax.broadcasted_iota(jnp.int32, (TOK, LANES), 1) // HEAD_DIM

    for group in range(3):
        at = group * LANES
        parts = []
        for win in range(2):
            rows = slice(win * TOK, win * TOK + TOK)
            parts.append(
                (
                    qkv_s[rows, at : at + LANES],
                    qkv_s[rows, D + at : D + at + LANES],
                    qkv_s[rows, 2 * D + at : 2 * D + at + LANES],
                    gm_s[rows, at : at + LANES],
                )
            )
        sums = [[jnp.zeros((TOK, LANES), WIDE) for _ in range(4)] for _ in range(2)]
        for member in range(4):
            head = group * 4 + member
            mine = lane_head == member
            bias = bias_ref[head, :, 0:TOK]
            pair = jnp.zeros((TOK, TOK), WIDE)
            for win in range(2):
                query, key, value, gm = parts[win]
                none = jnp.zeros_like(query)
                query = jnp.where(mine, query, none)
                value_h = jnp.where(mine, value, none)
                gm_h = jnp.where(mine, gm, none)
                key_h = jnp.where(mine, key, none)
                scores = nt(query, key) * scale + bias
                scores = jnp.where(fills[win] == 0.0, scores, fills[win])
                exponent = jnp.exp(scores - jnp.max(scores, axis=-1, keepdims=True))
                prob = (exponent / jnp.sum(exponent, axis=-1, keepdims=True)).astype(LOW)
                grad_attn = nt(gm_h, value)
                prob_wide = prob.astype(WIDE)
                weighted = prob_wide * grad_attn
                grad_scores = weighted - prob_wide * jnp.sum(weighted, axis=-1, keepdims=True)
                pair = pair + grad_scores
                low = grad_scores.astype(LOW)
                sums[win][0] += nn(prob, value_h)
                sums[win][1] += nn(low, key_h)
                sums[win][2] += tn(low, query)
                sums[win][3] += tn(prob, gm_h)
            pair_ref[head] = pair
        for win in range(2):
            rows = slice(win * TOK, win * TOK + TOK)
            mixed, gq, gk, gv = sums[win]
            mixed_s[rows, at : at + LANES] = mixed.astype(LOW)
            gqkv_s[rows, at : at + LANES] = (gq * scale).astype(LOW)
            gqkv_s[rows, D + at : D + at + LANES] = (gk * scale).astype(LOW)
            gqkv_s[rows, 2 * D + at : 2 * D + at + LANES] = gv.astype(LOW)

    mixed = mixed_s[...]
    band = 4 * D // lat_count
    share = band // lon_count
    for part in range(4):
        value = tn(cot, mixed) if part == 3 else tn(gqkv_s[:, part * D : part * D + D], normed)
        for i in range(lat_count // 4):
            at = position(part * (lat_count // 4) + i, lat_count)
            for n in range(lon_count):
                first = i * band + n * share
                wgrad_ref[at, n // 2, n % 2] = value[first : first + share].astype(LOW)
    branch = nt(mixed, out_w_ref[...]).astype(LOW).astype(WIDE)
    output = filled + branch
    grad_normed = nn(gqkv_s[...], qkv_w_ref[...]).astype(LOW).astype(WIDE)
    scaled = grad_normed * gain
    grad_filled = cot_wide + inv_std * (
        scaled
        - jnp.mean(scaled, axis=-1, keepdims=True)
        - standard * jnp.mean(scaled * standard, axis=-1, keepdims=True)
    )
    input_grad = jnp.where(masked, 0.0, grad_filled)
    vgrad_ref[...] = jnp.zeros((8, D), WIDE)
    vgrad_ref[0:1, :] = jnp.sum(grad_normed * standard, axis=0, keepdims=True)
    vgrad_ref[1:2, :] = jnp.sum(jnp.where(masked, grad_filled, 0.0), axis=0, keepdims=True)
    for quad, ref in enumerate((y0, y1, y2, y3)):
        for part, value in enumerate((output, input_grad)):
            both = [value[w * TOK + quad * PADDED : w * TOK + quad * PADDED + PADDED] for w in range(2)]
            ref[:, part * D : part * D + D] = jnp.concatenate(both, axis=0).astype(LOW)


def turn(pair_ref, turned):
    for head in range(HEADS):
        turned[:, head, :] = pair_ref[head]
    turned[:, HEADS:ROWS, :] = jnp.zeros((TOK, ROWS - HEADS, TOK), WIDE)


def table_sums(first, last, total, place_ref, turned):
    lane_at = lax.broadcasted_iota(jnp.int32, (LANES, TOK), 0)

    def step(block, total):
        for inner in range(8):
            row = block * 8 + inner
            place = place_ref[pl.ds(row, 1), 0:TOK]
            chunk = place >> 7
            hot = ((place & 127) == lane_at).astype(WIDE).astype(LOW)
            grad = turned[row]
            spread = jnp.concatenate([jnp.where(chunk == c, grad, 0.0) for c in range(CHUNKS)], axis=0)
            total = total + nt(spread.astype(LOW), hot)
        return total

    return lax.fori_loop(first, last, step, total)


def block_kernel(
    lat_count,
    lon_count,
    mask_ref,
    fields_hbm,
    cot_hbm,
    table_hbm,
    index_hbm,
    qkv_w_hbm,
    out_w_hbm,
    token_ref,
    gain_ref,
    output_ref,
    grad_ref,
    rows_ref,
    table_ref,
    vector_ref,
    fields_v,
    cot_v,
    table_v,
    index_v,
    qkv_w_v,
    out_w_v,
    load_sem,
    spread,
    held,
    leaving,
    arrived,
    padded_table,
    packed_ref,
    in_send,
    in_recv,
    bias_ref,
    place_ref,
    ys,
    terms_ref,
    vgrad_ref,
    pair_ref,
    qkv_s,
    gm_s,
    mixed_s,
    gqkv_s,
    landed,
    turned,
    pair_in,
    pair_sum,
    lon_in,
    lon_sum,
    lat_in,
    table_in,
    vec_in,
    vec_sum,
    vec_in_lat,
    quad_send,
    quad_recv,
    pair_send,
    pair_recv,
    lon_send,
    lon_recv,
    lat_send,
    lat_recv,
    table_send,
    table_recv,
    vec_send,
    vec_recv,
    vec_lat_send,
    vec_lat_recv,
):
    lat, lon = lax.axis_index("lat"), lax.axis_index("lon")
    half = lon_count // 2
    core, column = lon % 2, lon // 2

    def lat_at(step):
        return (lat + step + lat_count) % lat_count

    def lon_at(step):
        return (lon + step + lon_count) % lon_count

    barrier = pltpu.get_barrier_semaphore()
    friends = [(lat, lon_at(d)) for d in range(1, lon_count)]
    friends += [(lat_at(d), lon) for d in range(1, lat_count)]
    friends += [(lat_at(1), lon_at(1)), (lat_at(-1), lon_at(-1))]
    for friend in friends:
        pl.semaphore_signal(barrier, inc=1, device_id=friend, device_id_type=pl.DeviceIdType.MESH)
    pairs = (
        (fields_hbm, fields_v),
        (cot_hbm, cot_v),
        (table_hbm, table_v),
        (index_hbm, index_v),
        (qkv_w_hbm, qkv_w_v),
        (out_w_hbm, out_w_v),
    )
    loads = [pltpu.make_async_copy(src, dst, load_sem.at[i]) for i, (src, dst) in enumerate(pairs)]
    for each in loads:
        each.start()

    in_copies = enter(
        [(lat_at(-1), lon_at(-1)), (lat_at(-1), lon), (lat, lon_at(-1))],
        loads,
        mask_ref,
        fields_v,
        cot_v,
        table_v,
        index_v,
        bias_ref,
        place_ref,
        spread,
        held,
        leaving,
        arrived,
        padded_table,
        packed_ref,
        in_send,
        in_recv,
        lambda: pl.semaphore_wait(barrier, len(friends)),
    )
    loads[4].wait()
    loads[5].wait()
    y0, y1, y2, y3 = (ys.at[i] for i in range(4))
    attend(
        lat_count,
        lon_count,
        lat == lat_count - 1,
        leaving.at[3],
        arrived.at[2],
        arrived.at[1],
        arrived.at[0],
        token_ref,
        gain_ref,
        qkv_w_v,
        out_w_v,
        bias_ref,
        y0,
        y1,
        y2,
        y3,
        terms_ref,
        vgrad_ref,
        pair_ref,
        qkv_s,
        gm_s,
        mixed_s,
        gqkv_s,
    )

    members = lat_count // 2
    mine = (lat // 2 + lat) % 2
    halves = (1 - mine, mine)
    spans = [pl.ds(h * members, members) for h in halves]

    pair_copies = [
        remote(
            terms_ref.at[span, :, 1 - core],
            pair_in.at[span],
            pair_send.at[i],
            pair_recv.at[i],
            (lat, lon + 1 - 2 * core),
        )
        for i, span in enumerate(spans)
    ]
    for each in pair_copies:
        each.start()
    quads = [
        remote(y3, landed.at[0], quad_send.at[0], quad_recv.at[0], (lat_at(1), lon_at(1))),
        remote(y2, landed.at[1], quad_send.at[1], quad_recv.at[1], (lat_at(1), lon)),
        remote(y1, landed.at[2], quad_send.at[2], quad_recv.at[2], (lat, lon_at(1))),
    ]
    for each in quads:
        each.start()
    vec_in[lon] = vgrad_ref[...]
    vecs = []
    for d in range(1, lon_count):
        to = lon_at(d)
        vecs.append(remote(vgrad_ref, vec_in.at[lon], vec_send.at[to], vec_recv.at[lon], (lat, to)))
    for each in vecs:
        each.start()

    turn(pair_ref, turned)
    lon_copies = []
    for i in range(2):
        pair_copies[i].wait_recv()

        def add_pair(step, carry, base=halves[i] * members):
            row = base + step
            for m in range(half):
                own = terms_ref[row, m, core].astype(WIDE)
                pair_sum[m, row] = (own + pair_in[row, m].astype(WIDE)).astype(LOW)
            return carry

        lax.fori_loop(0, members, add_pair, 0)
        for d in range(1, half):
            to = (column + d) % half
            each = remote(
                pair_sum.at[to, spans[i]],
                lon_in.at[column, spans[i]],
                lon_send.at[i, to],
                lon_recv.at[i, column],
                (lat, 2 * to + core),
            )
            each.start()
            lon_copies.append(each)

    total = jnp.zeros((CHUNKS * ROWS, LANES), WIDE)
    lat_copies = []
    for i in range(2):
        total = table_sums(8 * i, 8 * i + 8, total, place_ref, turned)
        for d in range(1, half):
            source = (column + d) % half
            remote(
                pair_sum.at[source, spans[i]],
                lon_in.at[source, spans[i]],
                lon_send.at[i, source],
                lon_recv.at[i, source],
                (lat, 2 * source + core),
            ).wait_recv()

        def add_lon(step, carry, base=halves[i] * members):
            row = base + step
            value = pair_sum[column, row].astype(WIDE)
            for d in range(1, half):
                value = value + lon_in[(column + d) % half, row].astype(WIDE)
            lon_sum[row] = value.astype(LOW)
            return carry

        lax.fori_loop(0, members, add_lon, 0)
        for d in range(i, members):
            group = (lat // 2 + d) % members
            to = 2 * group + (group + halves[i]) % 2
            each = remote(
                lon_sum.at[halves[i] * members + group], lat_in.at[lat], lat_send.at[to], lat_recv.at[lat], (to, lon)
            )
            each.start()
            lat_copies.append(each)

    total = table_sums(16, TOK // 8, total, place_ref, turned)
    for c in range(CHUNKS):
        table_in[lon, :, c * LANES : c * LANES + LANES] = total[c * ROWS : c * ROWS + ROWS].astype(LOW)
    tables = []
    for d in range(1, lon_count):
        to = lon_at(d)
        tables.append(remote(table_in.at[lon], table_in.at[lon], table_send.at[to], table_recv.at[lon], (lat, to)))
    for each in tables:
        each.start()

    for d in range(1, lon_count):
        source = lon_at(d)
        remote(vgrad_ref, vec_in.at[source], vec_send.at[source], vec_recv.at[source], (lat, source)).wait_recv()
    vec = vec_in[0]
    for source in range(1, lon_count):
        vec = vec + vec_in[source]
    vec_sum[...] = vec
    vec_in_lat[lat] = vec
    vec_lats = []
    for d in range(1, lat_count):
        to = lat_at(d)
        vec_lats.append(remote(vec_sum, vec_in_lat.at[lat], vec_lat_send.at[to], vec_lat_recv.at[lat], (to, lon)))
    for each in vec_lats:
        each.start()

    for each in quads:
        each.wait_recv()
    for quad in range(3):
        held[quad] = landed[quad].astype(WIDE)
    held[3] = y0[...].astype(WIDE)
    unpack(held, spread, output_ref, grad_ref)

    for d in range(1, lon_count):
        source = lon_at(d)
        remote(
            table_in.at[source], table_in.at[source], table_send.at[source], table_recv.at[source], (lat, source)
        ).wait_recv()
    table = table_in[0].astype(WIDE)
    for source in range(1, lon_count):
        table = table + table_in[source].astype(WIDE)
    for head in range(HEADS):
        table_ref[head] = table[head : head + 1, 0:NBIAS]

    for d in range(1, lat_count):
        source = lat_at(d)
        remote(
            vec_sum, vec_in_lat.at[source], vec_lat_send.at[source], vec_lat_recv.at[source], (source, lon)
        ).wait_recv()
    vec = vec_in_lat[0]
    for source in range(1, lat_count):
        vec = vec + vec_in_lat[source]
    vector_ref[...] = vec[0:2]

    value = lon_sum[position(lat, lat_count)].astype(WIDE)
    for d in range(1, lat_count):
        source = lat_at(d)
        remote(lon_sum.at[0], lat_in.at[source], lat_send.at[source], lat_recv.at[source], (source, lon)).wait_recv()
        value = value + lat_in[source].astype(WIDE)
    rows_ref[...] = value

    for each in in_copies + pair_copies + quads + vecs + lon_copies + tables + lat_copies + vec_lats:
        each.wait_send()


def write_kernel(*refs):
    sources, targets, buffers, in_sems, out_sems = refs[:5], refs[5:10], refs[10:15], refs[15], refs[16]
    reads = [pltpu.make_async_copy(sources[i], buffers[i], in_sems.at[i]) for i in range(5)]
    writes = [pltpu.make_async_copy(buffers[i], targets[i], out_sems.at[i]) for i in range(5)]
    for each in reads:
        each.start()
    for i in range(5):
        reads[i].wait()
        writes[i].start()
    for each in writes:
        each.wait()


def struct(shape, dtype):
    return jax.ShapeDtypeStruct(shape, dtype)


def local(
    fields,
    cotangent,
    window_mask,
    mask_token,
    norm_gain,
    qkv_weight,
    out_weight,
    bias_table,
    bias_index,
):
    lat_count, lon_count = lax.axis_size("lat"), lax.axis_size("lon")
    half = lon_count // 2
    share = 4 * D // (lat_count * lon_count)

    def low(*shape):
        return pltpu.VMEM(shape, LOW)

    def wide(*shape):
        return pltpu.VMEM(shape, WIDE)

    def sems(*shape):
        return [pltpu.SemaphoreType.DMA(shape)] * 2

    output, input_grad, weight_grads, table_grad, vector_grads = pl.pallas_call(
        functools.partial(block_kernel, lat_count, lon_count),
        out_shape=(
            struct((6, 12, 4, D), LOW),
            struct((6, 12, 4, D), LOW),
            struct((share, D), WIDE),
            struct((HEADS, 1, NBIAS), WIDE),
            struct((2, D), WIDE),
        ),
        in_specs=[SMEM] + [HBM] * 6 + [VMEM] * 2,
        out_specs=(VMEM,) * 5,
        scratch_shapes=[
            low(6, 12, 4, D),
            low(6, 12, 4, D),
            wide(HEADS, 1, NBIAS),
            pltpu.VMEM((144, 144), jnp.int32),
            low(3 * D, D),
            low(D, D),
            pltpu.SemaphoreType.DMA((6,)),
            wide(2, 3, 288, LANES),
            wide(4, QUAD, 2 * D),
            low(4, QUAD, 2 * D),
            low(3, QUAD, 2 * D),
            wide(ROWS, CHUNKS * LANES),
            pltpu.VMEM((PADDED, LANES), jnp.int32),
            *sems(3),
            wide(HEADS, TOK, 2 * LANES),
            pltpu.VMEM((TOK, 2 * LANES), jnp.int32),
            low(4, QUAD, 2 * D),
            low(lat_count, half, 2, share, D),
            wide(8, D),
            wide(HEADS, TOK, TOK),
            low(2 * TOK, 3 * D),
            low(2 * TOK, D),
            low(2 * TOK, D),
            low(2 * TOK, 3 * D),
            low(3, QUAD, 2 * D),
            wide(TOK, ROWS, TOK),
            low(lat_count, half, share, D),
            low(half, lat_count, share, D),
            low(half, lat_count, share, D),
            low(lat_count, share, D),
            low(lat_count, share, D),
            low(lon_count, ROWS, CHUNKS * LANES),
            wide(lon_count, 8, D),
            wide(8, D),
            wide(lat_count, 8, D),
            *sems(3),
            *sems(2),
            *sems(2, half),
            *sems(lat_count),
            *sems(lon_count),
            *sems(lon_count),
            *sems(lat_count),
        ],
        compiler_params=pltpu.CompilerParams(
            collective_id=0, has_side_effects=True, vmem_limit_bytes=LIMIT
        ),
        name="block",
    )(
        window_mask.transpose(1, 2, 0),
        fields.transpose(1, 2, 0, 3),
        cotangent.transpose(1, 2, 0, 3),
        bias_table.transpose(1, 0, 2),
        bias_index,
        qkv_weight,
        out_weight,
        mask_token,
        norm_gain,
    )
    results = (output, input_grad, weight_grads, table_grad, vector_grads)
    output, input_grad, weight_grads, table_grad, vector_grads = pl.pallas_call(
        write_kernel,
        out_shape=tuple(struct(each.shape, each.dtype) for each in results),
        in_specs=[HBM] * 5,
        out_specs=(HBM,) * 5,
        scratch_shapes=[pltpu.VMEM(each.shape, each.dtype) for each in results] + sems(5),
        compiler_params=PARAMS,
        name="write",
    )(*results)
    output = output.transpose(2, 0, 1, 3)
    input_grad = input_grad.transpose(2, 0, 1, 3)
    table_grad = table_grad.transpose(1, 0, 2)
    return (output, input_grad, weight_grads, table_grad, vector_grads)


def solution(mesh):
    placed = (
        P(None, "lat", "lon", None),
        P(None, "lat", "lon", None),
        P(None, "lat", "lon"),
        P(),
        P(),
        P(),
        P(),
        P("lat", None, None),
        P(),
    )
    return jax.shard_map(
        local,
        mesh=mesh,
        in_specs=placed,
        out_specs=(
            P(None, "lat", "lon", None),
            P(None, "lat", "lon", None),
            P(("lat", "lon"), None),
            P("lat", None, None),
            P(),
        ),
        check_vma=False,
    )
```
